32 devices in a mesh: image: 2 (over x), orb: 16 (over z, y, core).
Axes of the slice: x: 2, y: 2, z: 4, core: 2. Of those that a mesh axis runs over, the one named last changes fastest.
Arguments:
- orb_blocks: bfloat16 [128, 256, 512], P(('image', 'orb')), parts along dimension 0, may hold values from -6 to 6
- pno: bfloat16 [1536, 200, 256], P(('image', 'orb')), parts along dimension 0, may hold values from -0.375 to 0.375
- pno_levels: float32 [1536, 200], P(('image', 'orb')), parts along dimension 0, may hold values from 0.5 to 4
- occ_levels: float32 [128], P(('image', 'orb')), parts along dimension 0, may hold values from -1.5 to -0.3
- pair_i_local: int32 [1536], P(('image', 'orb')), parts along dimension 0, may hold values from 0 to 3
- fetch_local: int32 [1024], P(('image', 'orb')), parts along dimension 0, may hold values from 0 to 3, as said below
- pair_slot: int32 [1536, 1], P(('image', 'orb')), parts along dimension 0, may hold values from 0 to 31; in each aligned block of 48 rows (0 to 47, 48 to 95, ...) at most 3 rows name the same one
Outputs:
- amplitudes: float32 [1536, 200, 200], P(('image', 'orb')), parts along dimension 0
- density: float32 [128, 256, 512], P(('image', 'orb')), parts along dimension 0
The draws below stay inside these ranges and needn't reach their ends.
There are 2 independent parts, one for each index of `image`. The reference program is written for one: setup_inputs(seed, part) draws one part's arguments, and reference() takes and returns one part's arrays. A program takes and returns all parts, laid end to end along the dimension named above; each array names one. Nothing has to cross between parts.
Inputs may be any that keep to these rules, and one draw needn't show every extreme that they name: `pair_slot`: within the 48 pairs of one device, no slot is named by more than 3 pairs; in some devices one slot is named by exactly 3. `fetch_local`: the 2 orbitals that one device asks of one owner are distinct.
All inputs are finite; a program needn't handle non-finite values.
Results may differ from the reference program's by a relative error of at most 0.0037.
Values may be sent and summed in bfloat16 or wider, within the bound.
A program may use at most 192 MiB of HBM per device.

```python
import math
import jax
import jax.numpy as jnp
import numpy as np
from jax import lax

AUX = 512
NVIRT = 256
NPNO = 200
ORB_DEV = 4
PAIR_DEV = 48
SLOTS = 32
MOST = 3
ITERS = 2
NOCC = 64
NPAIR = 768
N_ORB = 16


def draw_fetch_local(key, part):
    key = jax.random.fold_in(key, 11)
    groups = N_ORB * N_ORB
    scores = jax.random.randint(key, (groups, ORB_DEV), 0, 1 << 20) * ORB_DEV + jnp.arange(ORB_DEV, dtype=jnp.int32)[None, :]
    order = jnp.argsort(scores, axis=1, stable=True)
    return order[:, :SLOTS // N_ORB].reshape(-1).astype(jnp.int32)


def place_ends(entries, rng, low, top_value):
    longest = entries.shape.index(max(entries.shape))
    spots = []
    for shift in (0, 1):
        where = [jax.random.randint(jax.random.fold_in(rng, axis), (), 0, length) for axis, length in enumerate(entries.shape)]
        where[longest] = (where[longest] + shift) % entries.shape[longest]
        spots.append(tuple(where))
    return entries.at[spots[0]].set(low).at[spots[1]].set(top_value)


def levels(stream_key, shape, split, low, high):
    factor_of = 1.0
    for position, blocks in split:
        draws = jax.random.uniform(jax.random.fold_in(jax.random.fold_in(stream_key, 6), position), (blocks,), jnp.float32, low / len(split), high / len(split))
        factor_of = factor_of * jnp.repeat(jnp.exp(draws), shape[position] // blocks).reshape((-1,) + (1,) * (len(shape) - 1 - position))
    return factor_of


def deal_out(stream_key, own, number, rows, number_of, top, most, slope):
    sequence = jax.random.permutation(stream_key, number_of)
    crowded, common = shares(number_of, rows * top, most, slope, True), shares(number_of, rows * top, most, slope, False)
    places = jnp.arange(number_of)

    def named(sizes, turn):
        used = int((sizes > 0).sum())
        fixed = max(1, used // 4)
        passed = fixed + (places - fixed + turn * (used - fixed)) % max(1, number_of - fixed)
        return jnp.zeros((number_of,), jnp.int32).at[sequence[jnp.where(places < fixed, places, passed)]].set(jnp.asarray(sizes, jnp.int32))

    sizes = jnp.where(number % 4 == 0, named(crowded, number // 4), named(common, number - number // 4 - 1))
    mixed = jax.random.permutation(jax.random.fold_in(own, 3), number_of)
    donor, sink = mixed[0:number_of // 2 * 2:2], mixed[1:number_of // 2 * 2:2]
    room = jnp.minimum(sizes[donor] - 1, most - sizes[sink]) // 2
    room = jnp.where((donor == sequence[0]) | (sink == sequence[0]) | (sizes[sink] == 0), 0, jnp.maximum(room, 0))
    passed = jax.random.randint(jax.random.fold_in(own, 4), (number_of // 2,), 0, 1 << 20) % (room + 1)
    sizes = sizes.at[donor].add(-passed).at[sink].add(passed)
    members = jnp.searchsorted(jnp.cumsum(sizes), jnp.arange(rows * top), side="right").astype(jnp.int32)
    listing = members.reshape(top, rows).T
    listing = listing[jax.random.permutation(jax.random.fold_in(own, 1), rows)]
    turn = jax.random.randint(jax.random.fold_in(own, 2), (rows, 1), 0, top)
    return jnp.take_along_axis(listing, (jnp.arange(top)[None, :] + turn) % top, axis=1)


def shares(number_of, total, bound, slope, full):
    portions = [(1 << 20) // math.isqrt(standing ** slope) + 1 for standing in range(1, number_of + 1)]
    largest = bound if full else min(bound, max(-(-total // number_of), total * portions[0] // sum(portions)))
    least = 1 if total - largest >= number_of - 1 else 0
    given, spare = [largest] + [least] * (number_of - 1), total - largest - least * (number_of - 1)
    while spare > 0:
        movable = [i for i in range(1, number_of) if given[i] < largest] or [i for i in range(1, number_of) if given[i] < bound]
        pool, budget = sum([portions[i] for i in movable]), spare
        for i in movable:
            more = min(bound - given[i], max(1, budget * portions[i] // pool), spare)
            given[i] = given[i] + more
            spare = spare - more
    return np.array(given)


def noise(own_key, dims, scale, reach, pieces=(), held_as=jnp.bfloat16):
    entries = scale * jax.random.normal(own_key, dims, jnp.float32)
    if pieces:
        entries = entries * levels(own_key, dims, pieces, -0.22, 0.18)
    return jnp.clip(entries, -reach, reach).astype(held_as)


def setup_inputs(seed: int = 0, part: int = 0) -> dict:
    seeds = jax.random.split(jax.random.key(seed), 8)
    part_keys = jax.random.split(jax.random.fold_in(seeds[7], part), 8)
    orb_blocks = noise(part_keys[0], (NOCC, NVIRT, AUX), 1.0, 6.0, ((0, 16),))
    pno = noise(part_keys[1], (NPAIR, NPNO, NVIRT), NVIRT ** -0.5, 0.375, ((0, 16),))
    pno_levels = jnp.clip(jnp.exp(math.log(4.0) - 2.0794415 * jax.random.uniform(part_keys[2], (NPAIR, NPNO), jnp.float32) ** levels(part_keys[2], (NPAIR, NPNO), ((0, 16),), -0.2, 0.2)), 0.5, 4.0)
    occ_levels = jnp.clip(-1.5 + 1.2 * jax.random.uniform(part_keys[3], (NOCC,), jnp.float32) ** levels(part_keys[3], (NOCC,), ((0, 16),), -0.2, 0.2), -1.5, -0.3)
    pair_i_local = place_ends(jax.random.randint(part_keys[4], (NPAIR,), 0, ORB_DEV), jax.random.fold_in(part_keys[4], 1), 0, ORB_DEV - 1).astype(jnp.int32)
    fetch_local = draw_fetch_local(jax.random.fold_in(jax.random.fold_in(seeds[7], part), 71), part)
    pair_slot_keys = jax.random.split(jax.random.fold_in(part_keys[6], 1), NPAIR // PAIR_DEV)
    pair_slot_turns = jax.random.permutation(jax.random.fold_in(part_keys[6], 3), NPAIR // PAIR_DEV)
    pair_slot = jax.vmap(lambda own, number: deal_out(jax.random.fold_in(part_keys[6], 2), own, number, PAIR_DEV, SLOTS, 1, MOST, 1))(pair_slot_keys, pair_slot_turns).reshape((NPAIR, 1))
    return {"orb_blocks": orb_blocks, "pno": pno, "pno_levels": pno_levels, "occ_levels": occ_levels, "pair_i_local": pair_i_local, "fetch_local": fetch_local, "pair_slot": pair_slot}


shift_weight = 0.1


def reference(orb_blocks, pno, pno_levels, occ_levels, pair_i_local, fetch_local, pair_slot):
    pair_ids = jnp.arange(NPAIR, dtype=jnp.int32)
    per_owner = SLOTS // N_ORB
    device_of = (pair_ids // PAIR_DEV).astype(jnp.int32)
    slot_of = pair_slot[:, 0].astype(jnp.int32)
    first_orb = (device_of * ORB_DEV + pair_i_local).astype(jnp.int32)
    asked_index = (device_of * SLOTS + slot_of).astype(jnp.int32)
    second_orb = ((slot_of // per_owner) * ORB_DEV + fetch_local[asked_index]).astype(jnp.int32)
    integral_scale = AUX ** -0.5

    def projections(index):
        coeff = pno[index]
        first_proj = jnp.dot(coeff, orb_blocks[first_orb[index]], preferred_element_type=jnp.float32).astype(jnp.bfloat16)
        second_proj = jnp.dot(coeff, orb_blocks[second_orb[index]], preferred_element_type=jnp.float32).astype(jnp.bfloat16)
        return first_proj, second_proj

    def coulomb_of(index):
        first_proj, second_proj = projections(index)
        return jnp.dot(first_proj, second_proj.T, preferred_element_type=jnp.float32) * integral_scale

    coulomb = lax.map(coulomb_of, pair_ids)
    denominator = pno_levels[:, :, None] + pno_levels[:, None, :] - (occ_levels[first_orb] + occ_levels[second_orb])[:, None, None]
    amplitude = -coulomb / denominator
    for sweep in range(ITERS):
        pair_energy = jnp.sum(coulomb * (2.0 * amplitude - jnp.swapaxes(amplitude, 1, 2)), axis=(1, 2)) / (NPNO * NPNO)
        orbital_energy = jax.ops.segment_sum(pair_energy, first_orb, num_segments=NOCC) + jax.ops.segment_sum(pair_energy, second_orb, num_segments=NOCC)
        shifts = shift_weight * orbital_energy
        pair_shift = shifts[first_orb] + shifts[second_orb]
        residual = coulomb + (denominator + pair_shift[:, None, None]) * amplitude
        amplitude = amplitude - residual / denominator
    amp_half = amplitude.astype(jnp.bfloat16)

    def accumulate(total, index):
        coeff = pno[index]
        first_proj, second_proj = projections(index)
        first_part = jnp.dot(amp_half[index], second_proj, preferred_element_type=jnp.float32).astype(jnp.bfloat16)
        second_part = jnp.dot(amp_half[index].T, first_proj, preferred_element_type=jnp.float32).astype(jnp.bfloat16)
        first_pao = jnp.dot(coeff.T, first_part, preferred_element_type=jnp.float32).astype(jnp.bfloat16)
        second_pao = jnp.dot(coeff.T, second_part, preferred_element_type=jnp.float32).astype(jnp.bfloat16)
        total = total.at[first_orb[index]].add(first_pao.astype(jnp.float32))
        total = total.at[second_orb[index]].add(second_pao.astype(jnp.float32))
        return total, None

    density, unused = lax.scan(accumulate, jnp.zeros((NOCC, NVIRT, AUX), jnp.float32), pair_ids)
    return amplitude, density
```

```python
import functools

import jax
import jax.numpy as jnp
from jax import lax
from jax.experimental import pallas as pl
from jax.experimental.pallas import tpu as pltpu
from jax.sharding import PartitionSpec as P

ITERS = 2
shift_weight = 0.1
MESH = pl.DeviceIdType.MESH
F32 = jnp.float32
BF16 = jnp.bfloat16
VMEM_LIMIT = 56 * 1024 * 1024


def chip_at(position, chips):
    position = lax.rem(position + 2 * chips, chips)
    if chips == 8:
        far = position // 4
        return 2 * (position + far * (7 - 2 * position)) + far
    return position


def place_of(chip, chips):
    if chips == 8:
        y = lax.rem(chip, 2)
        z = chip // 2
        return z + y * (7 - 2 * z)
    return chip


def ring(n):
    me = lax.axis_index("orb")
    chips = n // 2
    core = lax.rem(me, 2)
    place = place_of(me // 2, chips)

    def dev(position, c):
        return chip_at(position, chips) * 2 + c

    return me, chips, core, place, dev


def greet(others):
    barrier = pltpu.get_barrier_semaphore()
    for other in others:
        pl.semaphore_signal(barrier, inc=1, device_id={"orb": other}, device_id_type=MESH)
    pl.semaphore_wait(barrier, len(others))


def remote(src, dst, send, recv, target):
    return pltpu.make_async_remote_copy(
        src_ref=src, dst_ref=dst, send_sem=send, recv_sem=recv, device_id={"orb": target}, device_id_type=MESH
    )


def gather_kernel(n, x_ref, info_ref, out_ref, info_out, ring_send, ring_recv, sib_send, sib_recv, info_send, info_recv, own_sem):
    me, chips, core, place, dev = ring(n)
    orbs = x_ref.shape[0]
    half = orbs // 2
    greet([lax.rem(me + d, n) for d in range(1, n)])
    ends = (dev(place + 1, core), dev(place - 1, core))
    sibling = me + 1 - 2 * core
    waits = []

    def row(position, way, k):
        return dev(position, core) * orbs + way * half + k

    arrivals = []
    for step in range(chips):
        incoming = []
        for k in range(half):
            for way in range(2):
                position = place - step if way == 0 else place + step
                r = row(position, way, k)
                if step == 0:
                    src = x_ref.at[way * half + k]
                else:
                    arrivals[step - 1][k * 2 + way].wait_recv()
                    src = out_ref.at[r]
                if step < chips - 1:
                    copy = remote(src, out_ref.at[r], ring_send.at[way, step, k], ring_recv.at[way, step, k], ends[way])
                    copy.start()
                    incoming.append(copy)
                    waits.append(copy.wait_send)
                side = remote(src, out_ref.at[r], sib_send.at[way, step, k], sib_recv.at[way, step, k], sibling)
                side.start()
                waits.append(side.wait_send)
                waits.append(side.wait_recv)
        arrivals.append(incoming)
        if step == 0:
            own = pltpu.make_async_copy(x_ref, out_ref.at[pl.ds(me * orbs, orbs)], own_sem.at[0])
            own.start()
            waits.append(own.wait)
            for d in range(1, n):
                note = remote(info_ref, info_out.at[me], info_send.at[d - 1], info_recv.at[d - 1], lax.rem(me + d, n))
                note.start()
                waits.append(note.wait_send)
                waits.append(note.wait_recv)
            info_out[me] = info_ref[...]
    for wait in waits:
        wait()


def gather(n, x, info):
    chips, half = n // 2, x.shape[0] // 2
    dma = pltpu.SemaphoreType.DMA
    return pl.pallas_call(
        functools.partial(gather_kernel, n),
        name="gather_blocks",
        out_shape=(
            jax.ShapeDtypeStruct((n * x.shape[0],) + x.shape[1:], x.dtype),
            jax.ShapeDtypeStruct((n,) + info.shape, info.dtype),
        ),
        in_specs=[pl.BlockSpec(memory_space=pl.ANY), pl.BlockSpec(memory_space=pltpu.VMEM)],
        out_specs=(pl.BlockSpec(memory_space=pl.ANY), pl.BlockSpec(memory_space=pltpu.VMEM)),
        scratch_shapes=[
            dma((2, chips, half)), dma((2, chips, half)), dma((2, chips, half)), dma((2, chips, half)),
            dma((n - 1,)), dma((n - 1,)), dma((1,)),
        ],
        compiler_params=pltpu.CompilerParams(collective_id=0, has_side_effects=True, vmem_limit_bytes=VMEM_LIMIT),
    )(x, info)


def coulomb_kernel(group, orbs, first_s, second_s, fglob_s, info_s, x_ref, pno_ref, level_ref, *rest):
    blocks = rest[:group]
    fp_ref, sp_ref, c_ref, e_ref = rest[group:]
    step = pl.program_id(0)
    width = pno_ref.shape[1]
    scale = x_ref.shape[2] ** -0.5
    lane = lax.broadcasted_iota(jnp.int32, (1, 128), 1)

    @pl.when(step == 0)
    def _():
        e_ref[...] = jnp.zeros_like(e_ref)
        e_ref[2:4, :] = jnp.full((2, 128), -1.0, F32)

    for j in range(group):
        p = step * group + j
        fg, sg = fglob_s[p], second_s[p]
        w = pno_ref[j]
        fp = jnp.dot(w, x_ref[first_s[p]], preferred_element_type=F32).astype(BF16)
        sp = jnp.dot(w, blocks[j][0], preferred_element_type=F32).astype(BF16)
        c = lax.dot_general(fp, sp, (((1,), (1,)), ((), ())), preferred_element_type=F32) * scale
        levels = jnp.broadcast_to(level_ref[0, j:j + 1, :], (width, width))
        occ = info_s[fg // orbs, lax.rem(fg, orbs)] + info_s[sg // orbs, lax.rem(sg, orbs)]
        inverse = 1.0 / (levels + levels.T - occ)
        t = c * (2.0 * c - c.T) * inverse
        norm = -1.0 / (width * width)
        e0 = jnp.sum(t) * norm
        e1 = jnp.sum(t * inverse) * norm
        fp_ref[j] = fp
        sp_ref[j] = sp
        c_ref[j] = c
        here = lane == p
        e_ref[0:1, :] = jnp.where(here, e0, e_ref[0:1, :])
        e_ref[1:2, :] = jnp.where(here, e1, e_ref[1:2, :])
        e_ref[2:3, :] = jnp.where(here, fg.astype(F32), e_ref[2:3, :])
        e_ref[3:4, :] = jnp.where(here, sg.astype(F32), e_ref[3:4, :])


def group_of(pairs):
    return next(g for g in (4, 3, 2, 1) if pairs % g == 0)


def coulomb_call(first_local, second, first_glob, info, x, gathered, pno, levels):
    pairs, width, nvirt = pno.shape
    aux = x.shape[2]
    group = group_of(pairs)

    def second_map(j, i, fl, sg, fg):
        return (sg[i * group + j], 0, 0)

    three = lambda i, *_: (i, 0, 0)
    zero3 = lambda i, *_: (0, 0, 0)
    return pl.pallas_call(
        functools.partial(coulomb_kernel, group, x.shape[0]),
        name="coulomb",
        out_shape=(
            jax.ShapeDtypeStruct((pairs, width, aux), BF16),
            jax.ShapeDtypeStruct((pairs, width, aux), BF16),
            jax.ShapeDtypeStruct((pairs, width, width), F32),
            jax.ShapeDtypeStruct((8, 128), F32),
        ),
        grid_spec=pltpu.PrefetchScalarGridSpec(
            num_scalar_prefetch=3,
            grid=(pairs // group,),
            in_specs=[
                pl.BlockSpec(memory_space=pltpu.SMEM),
                pl.BlockSpec(x.shape, zero3),
                pl.BlockSpec((group, width, nvirt), three),
                pl.BlockSpec((1, group, width), three),
            ] + [pl.BlockSpec((1, nvirt, aux), functools.partial(second_map, j)) for j in range(group)],
            out_specs=(
                pl.BlockSpec((group, width, aux), three),
                pl.BlockSpec((group, width, aux), three),
                pl.BlockSpec((group, width, width), three),
                pl.BlockSpec((8, 128), lambda i, *_: (0, 0)),
            ),
        ),
        compiler_params=pltpu.CompilerParams(vmem_limit_bytes=VMEM_LIMIT),
    )(first_local, second, first_glob, info, x, pno, levels.reshape(pairs // group, group, width), *([gathered] * group))


def shift_kernel(n, orb_total, e_ref, out_ref, got, send, recv):
    me = lax.axis_index("orb")
    greet([lax.rem(me + d, n) for d in range(1, n)])
    copies = []
    for d in range(1, n):
        copy = remote(e_ref, got.at[me], send.at[d - 1], recv.at[d - 1], lax.rem(me + d, n))
        copy.start()
        copies.append(copy)
    got[me] = e_ref[...]
    for copy in copies:
        copy.wait()
    ids = lax.broadcasted_iota(jnp.int32, (orb_total, 128), 0).astype(F32)

    def shares(block):
        return jnp.where(ids == block[2:3, :], 1.0, 0.0) + jnp.where(ids == block[3:4, :], 1.0, 0.0)

    total = jnp.zeros((orb_total, 128), F32)
    for d in range(n):
        block = got[d]
        total = total + shares(block) * block[0:1, :]
    shift = shift_weight * jnp.sum(total, axis=1, keepdims=True)
    total = jnp.zeros((orb_total, 128), F32)
    for d in range(n):
        block = got[d]
        hot = shares(block)
        pair_shift = jnp.sum(hot * shift, axis=0, keepdims=True)
        total = total + hot * (block[0:1, :] - pair_shift * block[1:2, :])
    shift2 = shift_weight * jnp.sum(total, axis=1, keepdims=True)
    mine = shares(e_ref[...])
    out_ref[...] = jnp.zeros_like(out_ref)
    out_ref[0:1, :] = jnp.sum(mine * shift, axis=0, keepdims=True)
    out_ref[1:2, :] = jnp.sum(mine * shift2, axis=0, keepdims=True)


def shift_call(n, orb_total, energies):
    dma = pltpu.SemaphoreType.DMA
    return pl.pallas_call(
        functools.partial(shift_kernel, n, orb_total),
        name="shifts",
        out_shape=jax.ShapeDtypeStruct((8, 128), F32),
        in_specs=[pl.BlockSpec(memory_space=pltpu.VMEM)],
        out_specs=pl.BlockSpec(memory_space=pltpu.VMEM),
        scratch_shapes=[pltpu.VMEM((n, 8, 128), F32), dma((n - 1,)), dma((n - 1,))],
        compiler_params=pltpu.CompilerParams(collective_id=1, has_side_effects=True, vmem_limit_bytes=VMEM_LIMIT),
    )(energies)


def density_kernel(group, orbs, first_s, slot_s, second_s, fglob_s, fresh_s, final_s, seen_s,
                   info_s, shift_s, pno_ref, level_ref, fp_ref, sp_ref, c_ref,
                   amp_ref, dens_ref, terms_ref, acc, stage, blank, busy, stage_sem, blank_sem):
    step = pl.program_id(0)
    width = pno_ref.shape[1]
    aux = fp_ref.shape[2]
    total = terms_ref.shape[0]

    def blank_copy(o):
        return pltpu.make_async_copy(blank, terms_ref.at[o], blank_sem.at[0])

    @pl.when(step == 0)
    def _():
        dens_ref[...] = jnp.zeros_like(dens_ref)
        blank[...] = jnp.zeros_like(blank)
        for j in range(group):
            busy[j] = 0

        @pl.loop(0, total)
        def _(o):
            @pl.when(seen_s[o] == 0)
            def _():
                blank_copy(o).start()

    for j in range(group):
        p = step * group + j
        fg, sg, slot = fglob_s[p], second_s[p], slot_s[p]
        levels = jnp.broadcast_to(level_ref[0, j:j + 1, :], (width, width))
        occ = info_s[fg // orbs, lax.rem(fg, orbs)] + info_s[sg // orbs, lax.rem(sg, orbs)]
        inverse = 1.0 / (levels + levels.T - occ)
        s1, s2 = shift_s[0, p], shift_s[1, p]
        amp = -c_ref[j] * inverse * (1.0 - s2 * inverse * (1.0 - s1 * inverse))
        amp_ref[j] = amp
        half = amp.astype(BF16)
        part1 = jnp.dot(half, sp_ref[j], preferred_element_type=F32).astype(BF16)
        part2 = lax.dot_general(half, fp_ref[j], (((0,), (0,)), ((), ())), preferred_element_type=F32).astype(BF16)
        parts = jnp.concatenate([part1, part2], axis=1)
        pao = lax.dot_general(pno_ref[j], parts, (((0,), (0,)), ((), ())), preferred_element_type=F32)
        dens_ref[first_s[p]] += pao[:, :aux]
        term = pao[:, aux:]
        acc[slot] = jnp.where(fresh_s[p] == 1, term, acc[slot] + term)

        @pl.when(final_s[p] == 1)
        def _():
            copy = pltpu.make_async_copy(stage.at[j], terms_ref.at[sg], stage_sem.at[j])

            @pl.when(busy[j] == 1)
            def _():
                copy.wait()

            stage[j] = acc[slot].astype(BF16)
            copy.start()
            busy[j] = 1

    @pl.when(step == pl.num_programs(0) - 1)
    def _():
        for j in range(group):
            @pl.when(busy[j] == 1)
            def _():
                pltpu.make_async_copy(stage.at[j], terms_ref.at[0], stage_sem.at[j]).wait()

        @pl.loop(0, total)
        def _(o):
            @pl.when(seen_s[o] == 0)
            def _():
                blank_copy(o).wait()


def density_call(scalars, info, shifts, orbs, slots, orb_total, pno, levels, fp, sp, c):
    pairs, width, nvirt = pno.shape
    aux = fp.shape[2]
    group = group_of(pairs)
    three = lambda i, *_: (i, 0, 0)
    smem = pl.BlockSpec(memory_space=pltpu.SMEM)
    dma = pltpu.SemaphoreType.DMA
    return pl.pallas_call(
        functools.partial(density_kernel, group, orbs),
        name="density_terms",
        out_shape=(
            jax.ShapeDtypeStruct((pairs, width, width), F32),
            jax.ShapeDtypeStruct((orbs, nvirt, aux), F32),
            jax.ShapeDtypeStruct((orb_total, nvirt, aux), BF16),
        ),
        grid_spec=pltpu.PrefetchScalarGridSpec(
            num_scalar_prefetch=7,
            grid=(pairs // group,),
            in_specs=[
                smem, smem,
                pl.BlockSpec((group, width, nvirt), three),
                pl.BlockSpec((1, group, width), three),
                pl.BlockSpec((group, width, aux), three),
                pl.BlockSpec((group, width, aux), three),
                pl.BlockSpec((group, width, width), three),
            ],
            out_specs=(
                pl.BlockSpec((group, width, width), three),
                pl.BlockSpec((orbs, nvirt, aux), lambda i, *_: (0, 0, 0)),
                pl.BlockSpec(memory_space=pl.ANY),
            ),
            scratch_shapes=[
                pltpu.VMEM((slots, nvirt, aux), F32),
                pltpu.VMEM((group, nvirt, aux), BF16),
                pltpu.VMEM((nvirt, aux), BF16),
                pltpu.SMEM((group,), jnp.int32),
                dma((group,)), dma((1,)),
            ],
        ),
        compiler_params=pltpu.CompilerParams(vmem_limit_bytes=VMEM_LIMIT),
    )(*scalars, info, shifts, pno, levels.reshape(pairs // group, group, width), fp, sp, c)


def home_kernel(n, terms_ref, dens_ref, out_ref, own, side, got, own_sem, side_send, side_recv, ring_send, ring_recv):
    me, chips, core, place, dev = ring(n)
    orbs, rows = dens_ref.shape[0], dens_ref.shape[1]
    half = orbs // 2
    sibling = me + 1 - 2 * core
    ends = (dev(place + 1, core), dev(place - 1, core))
    greet([ends[0], ends[1], sibling])
    chunk = 32

    def position(way, step):
        return place - 1 - step if way == 0 else place + 1 + step

    def own_copy(way, step, k):
        r = dev(position(way, step), core) * orbs + way * half + k
        return pltpu.make_async_copy(terms_ref.at[r], own.at[way, step, k], own_sem.at[way, step, k])

    def side_copy(way, step, k):
        r = dev(position(way, step), 1 - core) * orbs + way * half + k
        return remote(terms_ref.at[r], side.at[way, step, k], side_send.at[way, step, k], side_recv.at[way, step, k], sibling)

    def load(step):
        for k in range(half):
            for way in range(2):
                side_copy(way, step, k).start()
                own_copy(way, step, k).start()

    def ring_copy(way, step, k):
        return remote(side.at[way, step, k], got.at[way, step, k], ring_send.at[way, step, k], ring_recv.at[way, step, k], ends[way])

    load(0)
    load(1)
    for step in range(chips):
        for k in range(half):
            for way in range(2):
                own_copy(way, step, k).wait()
                side_copy(way, step, k).wait_recv()
                if step > 0:
                    ring_copy(way, step - 1, k).wait_recv()

                @pl.loop(0, rows // chunk)
                def _(i):
                    at = pl.ds(pl.multiple_of(i * chunk, chunk), chunk)
                    total = own[way, step, k, at, :].astype(F32) + side[way, step, k, at, :].astype(F32)
                    if step > 0:
                        total = total + got[way, step - 1, k, at, :].astype(F32)
                    if step < chips - 1:
                        side[way, step, k, at, :] = total.astype(BF16)
                    else:
                        out_ref[way * half + k, at, :] = dens_ref[way * half + k, at, :] + total

                if step < chips - 1:
                    ring_copy(way, step, k).start()
        if step + 2 < chips:
            load(step + 2)
    for step in range(chips):
        for k in range(half):
            for way in range(2):
                side_copy(way, step, k).wait_send()
                if step < chips - 1:
                    ring_copy(way, step, k).wait_send()


def home(n, terms, density):
    orbs, nvirt, aux = density.shape
    chips, half = n // 2, orbs // 2
    dma = pltpu.SemaphoreType.DMA
    many = (2, chips, half)
    return pl.pallas_call(
        functools.partial(home_kernel, n),
        name="terms_home",
        out_shape=jax.ShapeDtypeStruct(density.shape, F32),
        in_specs=[pl.BlockSpec(memory_space=pl.ANY), pl.BlockSpec(memory_space=pltpu.VMEM)],
        out_specs=pl.BlockSpec(memory_space=pltpu.VMEM),
        scratch_shapes=[
            pltpu.VMEM(many + (nvirt, aux), BF16),
            pltpu.VMEM(many + (nvirt, aux), BF16),
            pltpu.VMEM((2, chips - 1, half, nvirt, aux), BF16),
            dma(many), dma(many), dma(many), dma(many), dma(many),
        ],
        compiler_params=pltpu.CompilerParams(collective_id=2, has_side_effects=True, vmem_limit_bytes=VMEM_LIMIT),
    )(terms, density)


def on_device(orb_blocks, pno, pno_levels, occ_levels, pair_i_local, fetch_local, pair_slot):
    n = lax.axis_size("orb")
    orbs = orb_blocks.shape[0]
    pairs = pno.shape[0]
    slots = fetch_local.shape[0]
    orb_total = orbs * n
    per_owner = slots // n
    slot_of = pair_slot[:, 0]
    slot_ids = jnp.arange(slots, dtype=jnp.int32)
    pair_ids = jnp.arange(pairs, dtype=jnp.int32)
    slot_orb = slot_ids // per_owner * orbs + fetch_local
    first_glob = lax.axis_index("orb") * orbs + pair_i_local
    second = jnp.sum(jnp.where(slot_of[:, None] == slot_ids[None, :], slot_orb[None, :], 0), axis=1)
    same = slot_of[:, None] == slot_of[None, :]
    fresh = 1 - jnp.any(same & (pair_ids[None, :] < pair_ids[:, None]), axis=1).astype(jnp.int32)
    final = 1 - jnp.any(same & (pair_ids[None, :] > pair_ids[:, None]), axis=1).astype(jnp.int32)
    seen = jnp.any(second[:, None] == jnp.arange(orb_total, dtype=jnp.int32)[None, :], axis=0).astype(jnp.int32)
    info = jnp.pad(occ_levels[None, :], ((0, 7), (0, 128 - orbs)))
    gathered, info_all = gather(n, orb_blocks, info)
    info_all = info_all[:, 0, :orbs]
    fp, sp, coulomb, energies = coulomb_call(
        pair_i_local, second, first_glob, info_all, orb_blocks, gathered, pno, pno_levels
    )
    shifts = shift_call(n, orb_total, energies)
    scalars = (pair_i_local, slot_of, second, first_glob, fresh, final, seen)
    amplitude, density, terms = density_call(
        scalars, info_all, shifts, orbs, slots, orb_total, pno, pno_levels, fp, sp, coulomb
    )
    return (amplitude, home(n, terms, density))


def solution(mesh):
    placed = (
        P(("image", "orb"), None, None),
        P(("image", "orb"), None, None),
        P(("image", "orb"), None),
        P(("image", "orb")),
        P(("image", "orb")),
        P(("image", "orb")),
        P(("image", "orb"), None),
    )
    return jax.shard_map(
        on_device,
        mesh=mesh,
        in_specs=placed,
        out_specs=(P(("image", "orb"), None, None), P(("image", "orb"), None, None)),
        check_vma=False,
    )
```

```python
import functools

import jax
import jax.numpy as jnp
from jax import lax
from jax.experimental import pallas as pl
from jax.experimental.pallas import tpu as pltpu
from jax.sharding import PartitionSpec as P

MOST = 3
ITERS = 2
shift_weight = 0.1
MESH = pl.DeviceIdType.MESH
F32 = jnp.float32
BF16 = jnp.bfloat16
VMEM_LIMIT = 56 * 1024 * 1024


def chip_at(position, chips):
    position = lax.rem(position + 2 * chips, chips)
    if chips == 8:
        far = position // 4
        return 2 * (position + far * (7 - 2 * position)) + far
    return position


def place_of(chip, chips):
    if chips == 8:
        y = lax.rem(chip, 2)
        z = chip // 2
        return z + y * (7 - 2 * z)
    return chip


def ring(n):
    me = lax.axis_index("orb")
    chips = n // 2
    core = lax.rem(me, 2)
    place = place_of(me // 2, chips)

    def dev(position, c):
        return chip_at(position, chips) * 2 + c

    return me, chips, core, place, dev


def greet(others):
    barrier = pltpu.get_barrier_semaphore()
    for other in others:
        pl.semaphore_signal(barrier, inc=1, device_id={"orb": other}, device_id_type=MESH)
    pl.semaphore_wait(barrier, len(others))


def remote(src, dst, send, recv, target):
    return pltpu.make_async_remote_copy(
        src_ref=src, dst_ref=dst, send_sem=send, recv_sem=recv, device_id={"orb": target}, device_id_type=MESH
    )


def gather_kernel(n, per_owner, first_s, fetch_s, row_s, x_ref, pno_ref, level_ref, info_ref,
                  fp_out, sp_out, c_out, e_ref, info_out,
                  blocks, current, fp_stage, sp_stage, c_stage,
                  own_sem, first_send, first_recv, ring_send, ring_recv, side_send, side_recv, info_send, info_recv, out_sem):
    me, chips, core, place, dev = ring(n)
    orbs = x_ref.shape[0]
    half = orbs // 2
    width = pno_ref.shape[1]
    rows = per_owner * MOST
    scale = x_ref.shape[2] ** -0.5
    norm = -1.0 / (width * width)
    sibling = me + 1 - 2 * core
    ends = (dev(place + 1, core), dev(place - 1, core))
    lane = lax.broadcasted_iota(jnp.int32, (1, 128), 1)
    greet([lax.rem(me + d, n) for d in range(1, n)])

    def owner_at(way, step):
        return dev(place - step if way == 0 else place + step, way)

    def first_copy(k):
        local = lax.rem(half * (1 - core) + k, orbs)
        return remote(x_ref.at[local], blocks.at[me, local], first_send.at[k], first_recv.at[k], sibling)

    def ring_copy(way, step, k):
        block = blocks.at[owner_at(way, step - 1), half * core + k]
        return remote(block, block, ring_send.at[way, step, k], ring_recv.at[way, step, k], ends[way])

    def ring_wait(way, step, k):
        block = blocks.at[owner_at(way, step), half * core + k]
        remote(block, block, ring_send.at[way, step, k], ring_recv.at[way, step, k], ends[way]).wait_recv()

    def side_copy(way, step, k):
        block = blocks.at[owner_at(way, step), half * core + k]
        return remote(block, block, side_send.at[way, step, k], side_recv.at[way, step, k], sibling)

    def side_wait(way, step, k):
        block = blocks.at[owner_at(way, step), half * (1 - core) + k]
        remote(block, block, side_send.at[way, step, k], side_recv.at[way, step, k], sibling).wait_recv()

    def note(d):
        return remote(info_ref, info_out.at[me], info_send.at[d - 1], info_recv.at[d - 1], lax.rem(me + d, n))

    def out_copies(way, owner, i):
        row = owner * rows + i
        return [
            pltpu.make_async_copy(stage.at[way, i], out.at[row], out_sem.at[way, kind, i])
            for kind, (stage, out) in enumerate(((fp_stage, fp_out), (sp_stage, sp_out), (c_stage, c_out)))
        ]

    def work(way, step):
        owner = owner_at(way, step)
        for s in range(per_owner):
            local = fetch_s[owner * per_owner + s]
            block = blocks[owner, 0]
            for other in range(1, orbs):
                block = jnp.where(local == other, blocks[owner, other], block)
            current[...] = block
            occ2 = jnp.sum(jnp.where(lane == local, info_out[owner, 0:1, :], 0.0), axis=1, keepdims=True)
            for m in range(MOST):
                i = s * MOST + m
                row = owner * rows + i
                named = row_s[row]
                q = jnp.maximum(named, 0)
                first = first_s[q]
                w = pno_ref[q]
                fp = jnp.dot(w, x_ref[first], preferred_element_type=F32).astype(BF16)
                sp = jnp.dot(w, current[...], preferred_element_type=F32).astype(BF16)
                c = lax.dot_general(fp, sp, (((1,), (1,)), ((), ())), preferred_element_type=F32) * scale
                levels = jnp.broadcast_to(level_ref[q], (width, width))
                occ1 = jnp.sum(jnp.where(lane == first, info_ref[0:1, :], 0.0), axis=1, keepdims=True)
                inverse = 1.0 / (levels + levels.T - (occ1 + occ2))
                t = c * (2.0 * c - c.T) * inverse
                e0 = jnp.sum(t) * norm
                e1 = jnp.sum(t * inverse) * norm
                fp_stage[way, i] = fp
                sp_stage[way, i] = sp
                c_stage[way, i] = c
                for copy in out_copies(way, owner, i):
                    copy.start()
                here = lane == row
                id1 = jnp.where(named >= 0, me * orbs + first, -1).astype(F32)
                id2 = jnp.where(named >= 0, owner * orbs + local, -1).astype(F32)
                e_ref[0:1, :] = jnp.where(here, e0, e_ref[0:1, :])
                e_ref[1:2, :] = jnp.where(here, e1, e_ref[1:2, :])
                e_ref[2:3, :] = jnp.where(here, id1, e_ref[2:3, :])
                e_ref[3:4, :] = jnp.where(here, id2, e_ref[3:4, :])

    for k in range(orbs):
        first_copy(k).start()
    own = pltpu.make_async_copy(x_ref, blocks.at[me], own_sem.at[0])
    own.start()
    own.wait()
    for k in range(half):
        first_copy(k).wait_recv()
    for k in range(half):
        for way in range(2):
            ring_copy(way, 1, k).start()
    for d in range(1, n):
        note(d).start()
    info_out[me] = info_ref[...]
    e_ref[...] = jnp.zeros_like(e_ref)
    e_ref[2:4, :] = jnp.full((2, 128), -1.0, F32)
    for k in range(half, orbs):
        first_copy(k).wait_recv()
    for d in range(1, n):
        note(d).wait()

    def turn(step, carry):
        for k in range(half):
            @pl.when(step < chips)
            def _():
                for way in range(2):
                    ring_wait(way, step, k)

                    @pl.when(step < chips - 1)
                    def _():
                        ring_copy(way, step + 1, k).start()

                    side_copy(way, step, k).start()

            for way in range(2):
                if way % half == k:
                    @pl.when(step > 1)
                    def _():
                        for kk in range(half):
                            side_wait(way, step - 1, kk)
                        for i in range(rows):
                            for copy in out_copies(way, owner_at(way, step - 2), i):
                                copy.wait()

                    work(way, step - 1)
        return carry

    lax.fori_loop(1, chips + 1, turn, 0)
    for way in range(2):
        for i in range(rows):
            for copy in out_copies(way, owner_at(way, chips - 1), i):
                copy.wait()
    for k in range(orbs):
        first_copy(k).wait_send()

    def drain(step, carry):
        for k in range(half):
            for way in range(2):
                ring_copy(way, step, k).wait_send()
                side_copy(way, step, k).wait_send()
        return carry

    lax.fori_loop(1, chips, drain, 0)


def gather(n, first_local, fetch_local, row_pair, x, pno, levels, info):
    pairs, width, nvirt = pno.shape
    orbs, _, aux = x.shape
    per_owner = fetch_local.shape[0] // n
    rows = per_owner * MOST
    total = rows * n
    chips, half = n // 2, orbs // 2
    dma = pltpu.SemaphoreType.DMA
    smem, vmem, anywhere = (pl.BlockSpec(memory_space=m) for m in (pltpu.SMEM, pltpu.VMEM, pl.ANY))
    return pl.pallas_call(
        functools.partial(gather_kernel, n, per_owner),
        name="gather_coulomb",
        out_shape=(
            jax.ShapeDtypeStruct((total, width, aux), BF16),
            jax.ShapeDtypeStruct((total, width, aux), BF16),
            jax.ShapeDtypeStruct((total, width, width), F32),
            jax.ShapeDtypeStruct((8, 128), F32),
            jax.ShapeDtypeStruct((n,) + info.shape, info.dtype),
        ),
        in_specs=[smem, smem, smem, vmem, vmem, vmem, vmem],
        out_specs=(anywhere, anywhere, anywhere, vmem, vmem),
        scratch_shapes=[
            pltpu.VMEM((n, orbs, nvirt, aux), BF16),
            pltpu.VMEM((nvirt, aux), BF16),
            pltpu.VMEM((2, rows, width, aux), BF16),
            pltpu.VMEM((2, rows, width, aux), BF16),
            pltpu.VMEM((2, rows, width, width), F32),
            dma((1,)), dma((orbs,)), dma((orbs,)),
            dma((2, chips, half)), dma((2, chips, half)), dma((2, chips, half)), dma((2, chips, half)),
            dma((n - 1,)), dma((n - 1,)), dma((2, 3, rows)),
        ],
        compiler_params=pltpu.CompilerParams(collective_id=0, has_side_effects=True, vmem_limit_bytes=VMEM_LIMIT),
    )(first_local, fetch_local, row_pair, x, pno, levels.reshape(pairs, 1, width), info)


def group_of(pairs):
    return next(g for g in (4, 3, 2, 1) if pairs % g == 0)


def shift_kernel(n, orb_total, e_ref, out_ref, got, send, recv):
    me = lax.axis_index("orb")
    greet([lax.rem(me + d, n) for d in range(1, n)])
    copies = []
    for d in range(1, n):
        copy = remote(e_ref, got.at[me], send.at[d - 1], recv.at[d - 1], lax.rem(me + d, n))
        copy.start()
        copies.append(copy)
    got[me] = e_ref[...]
    for copy in copies:
        copy.wait()
    ids = lax.broadcasted_iota(jnp.int32, (orb_total, 128), 0).astype(F32)

    def shares(block):
        return jnp.where(ids == block[2:3, :], 1.0, 0.0) + jnp.where(ids == block[3:4, :], 1.0, 0.0)

    total = jnp.zeros((orb_total, 128), F32)
    for d in range(n):
        block = got[d]
        total = total + shares(block) * block[0:1, :]
    shift = shift_weight * jnp.sum(total, axis=1, keepdims=True)
    total = jnp.zeros((orb_total, 128), F32)
    for d in range(n):
        block = got[d]
        hot = shares(block)
        pair_shift = jnp.sum(hot * shift, axis=0, keepdims=True)
        total = total + hot * (block[0:1, :] - pair_shift * block[1:2, :])
    shift2 = shift_weight * jnp.sum(total, axis=1, keepdims=True)
    mine = shares(e_ref[...])
    out_ref[...] = jnp.zeros_like(out_ref)
    out_ref[0:1, :] = jnp.sum(mine * shift, axis=0, keepdims=True)
    out_ref[1:2, :] = jnp.sum(mine * shift2, axis=0, keepdims=True)


def shift_call(n, orb_total, energies):
    dma = pltpu.SemaphoreType.DMA
    return pl.pallas_call(
        functools.partial(shift_kernel, n, orb_total),
        name="shifts",
        out_shape=jax.ShapeDtypeStruct((8, 128), F32),
        in_specs=[pl.BlockSpec(memory_space=pltpu.VMEM)],
        out_specs=pl.BlockSpec(memory_space=pltpu.VMEM),
        scratch_shapes=[pltpu.VMEM((n, 8, 128), F32), dma((n - 1,)), dma((n - 1,))],
        compiler_params=pltpu.CompilerParams(collective_id=1, has_side_effects=True, vmem_limit_bytes=VMEM_LIMIT),
    )(energies)


def density_kernel(group, orbs, first_s, slot_s, second_s, fglob_s, fresh_s, final_s, seen_s, row_s,
                   info_s, shift_s, pno_ref, level_ref, *rest):
    fp_refs, sp_refs, c_refs = rest[:group], rest[group:2 * group], rest[2 * group:3 * group]
    amp_ref, dens_ref, terms_ref, acc, stage, blank, busy, stage_sem, blank_sem = rest[3 * group:]
    step = pl.program_id(0)
    width = pno_ref.shape[1]
    aux = fp_refs[0].shape[2]
    total = terms_ref.shape[0]

    def blank_copy(o):
        return pltpu.make_async_copy(blank, terms_ref.at[o], blank_sem.at[0])

    @pl.when(step == 0)
    def _():
        dens_ref[...] = jnp.zeros_like(dens_ref)
        blank[...] = jnp.zeros_like(blank)
        for j in range(group):
            busy[j] = 0

        @pl.loop(0, total)
        def _(o):
            @pl.when(seen_s[o] == 0)
            def _():
                blank_copy(o).start()

    for j in range(group):
        p = step * group + j
        fg, sg, slot = fglob_s[p], second_s[p], slot_s[p]
        levels = jnp.broadcast_to(level_ref[0, j:j + 1, :], (width, width))
        occ = info_s[fg // orbs, lax.rem(fg, orbs)] + info_s[sg // orbs, lax.rem(sg, orbs)]
        inverse = 1.0 / (levels + levels.T - occ)
        s1, s2 = shift_s[0, row_s[p]], shift_s[1, row_s[p]]
        amp = -c_refs[j][0] * inverse * (1.0 - s2 * inverse * (1.0 - s1 * inverse))
        amp_ref[j] = amp
        half = amp.astype(BF16)
        part1 = jnp.dot(half, sp_refs[j][0], preferred_element_type=F32).astype(BF16)
        part2 = lax.dot_general(half, fp_refs[j][0], (((0,), (0,)), ((), ())), preferred_element_type=F32).astype(BF16)
        parts = jnp.concatenate([part1, part2], axis=1)
        pao = lax.dot_general(pno_ref[j], parts, (((0,), (0,)), ((), ())), preferred_element_type=F32)
        dens_ref[first_s[p]] += pao[:, :aux]
        term = pao[:, aux:]
        acc[slot] = jnp.where(fresh_s[p] == 1, term, acc[slot] + term)

        @pl.when(final_s[p] == 1)
        def _():
            copy = pltpu.make_async_copy(stage.at[j], terms_ref.at[sg], stage_sem.at[j])

            @pl.when(busy[j] == 1)
            def _():
                copy.wait()

            stage[j] = acc[slot].astype(BF16)
            copy.start()
            busy[j] = 1

    @pl.when(step == pl.num_programs(0) - 1)
    def _():
        for j in range(group):
            @pl.when(busy[j] == 1)
            def _():
                pltpu.make_async_copy(stage.at[j], terms_ref.at[0], stage_sem.at[j]).wait()

        @pl.loop(0, total)
        def _(o):
            @pl.when(seen_s[o] == 0)
            def _():
                blank_copy(o).wait()


def density_call(scalars, info, shifts, orbs, slots, orb_total, pno, levels, fp, sp, c):
    pairs, width, nvirt = pno.shape
    aux = fp.shape[2]
    group = group_of(pairs)
    three = lambda i, *_: (i, 0, 0)

    def row_map(j, i, *scalars):
        return (scalars[-1][i * group + j], 0, 0)

    def picked(array):
        return [pl.BlockSpec((1,) + array.shape[1:], functools.partial(row_map, j)) for j in range(group)]

    smem = pl.BlockSpec(memory_space=pltpu.SMEM)
    dma = pltpu.SemaphoreType.DMA
    return pl.pallas_call(
        functools.partial(density_kernel, group, orbs),
        name="density_terms",
        out_shape=(
            jax.ShapeDtypeStruct((pairs, width, width), F32),
            jax.ShapeDtypeStruct((orbs, nvirt, aux), F32),
            jax.ShapeDtypeStruct((orb_total, nvirt, aux), BF16),
        ),
        grid_spec=pltpu.PrefetchScalarGridSpec(
            num_scalar_prefetch=8,
            grid=(pairs // group,),
            in_specs=[
                smem, smem,
                pl.BlockSpec((group, width, nvirt), three),
                pl.BlockSpec((1, group, width), three),
            ] + picked(fp) + picked(sp) + picked(c),
            out_specs=(
                pl.BlockSpec((group, width, width), three),
                pl.BlockSpec((orbs, nvirt, aux), lambda i, *_: (0, 0, 0)),
                pl.BlockSpec(memory_space=pl.ANY),
            ),
            scratch_shapes=[
                pltpu.VMEM((slots, nvirt, aux), F32),
                pltpu.VMEM((group, nvirt, aux), BF16),
                pltpu.VMEM((nvirt, aux), BF16),
                pltpu.SMEM((group,), jnp.int32),
                dma((group,)), dma((1,)),
            ],
        ),
        compiler_params=pltpu.CompilerParams(vmem_limit_bytes=VMEM_LIMIT),
    )(*scalars, info, shifts, pno, levels.reshape(pairs // group, group, width), *([fp] * group + [sp] * group + [c] * group))


def home_kernel(n, terms_ref, dens_ref, out_ref, own, side, got, own_sem, side_send, side_recv, ring_send, ring_recv):
    me, chips, core, place, dev = ring(n)
    orbs, rows = dens_ref.shape[0], dens_ref.shape[1]
    half = orbs // 2
    sibling = me + 1 - 2 * core
    ends = (dev(place + 1, core), dev(place - 1, core))
    greet([ends[0], ends[1], sibling])
    chunk = 32

    def position(way, step):
        return place - 1 - step if way == 0 else place + 1 + step

    def own_copy(way, step, k):
        r = dev(position(way, step), core) * orbs + way * half + k
        return pltpu.make_async_copy(terms_ref.at[r], own.at[way, step, k], own_sem.at[way, step, k])

    def side_copy(way, step, k):
        r = dev(position(way, step), 1 - core) * orbs + way * half + k
        return remote(terms_ref.at[r], side.at[way, step, k], side_send.at[way, step, k], side_recv.at[way, step, k], sibling)

    def load(step):
        for k in range(half):
            for way in range(2):
                side_copy(way, step, k).start()
                own_copy(way, step, k).start()

    def ring_copy(way, step, k):
        return remote(side.at[way, step, k], got.at[way, step, k], ring_send.at[way, step, k], ring_recv.at[way, step, k], ends[way])

    load(0)
    load(1)
    for step in range(chips):
        for k in range(half):
            for way in range(2):
                own_copy(way, step, k).wait()
                side_copy(way, step, k).wait_recv()
                if step > 0:
                    ring_copy(way, step - 1, k).wait_recv()

                @pl.loop(0, rows // chunk)
                def _(i):
                    at = pl.ds(pl.multiple_of(i * chunk, chunk), chunk)
                    total = own[way, step, k, at, :].astype(F32) + side[way, step, k, at, :].astype(F32)
                    if step > 0:
                        total = total + got[way, step - 1, k, at, :].astype(F32)
                    if step < chips - 1:
                        side[way, step, k, at, :] = total.astype(BF16)
                    else:
                        out_ref[way * half + k, at, :] = dens_ref[way * half + k, at, :] + total

                if step < chips - 1:
                    ring_copy(way, step, k).start()
        if step + 2 < chips:
            load(step + 2)
    for step in range(chips):
        for k in range(half):
            for way in range(2):
                side_copy(way, step, k).wait_send()
                if step < chips - 1:
                    ring_copy(way, step, k).wait_send()


def home(n, terms, density):
    orbs, nvirt, aux = density.shape
    chips, half = n // 2, orbs // 2
    dma = pltpu.SemaphoreType.DMA
    many = (2, chips, half)
    return pl.pallas_call(
        functools.partial(home_kernel, n),
        name="terms_home",
        out_shape=jax.ShapeDtypeStruct(density.shape, F32),
        in_specs=[pl.BlockSpec(memory_space=pl.ANY), pl.BlockSpec(memory_space=pltpu.VMEM)],
        out_specs=pl.BlockSpec(memory_space=pltpu.VMEM),
        scratch_shapes=[
            pltpu.VMEM(many + (nvirt, aux), BF16),
            pltpu.VMEM(many + (nvirt, aux), BF16),
            pltpu.VMEM((2, chips - 1, half, nvirt, aux), BF16),
            dma(many), dma(many), dma(many), dma(many), dma(many),
        ],
        compiler_params=pltpu.CompilerParams(collective_id=2, has_side_effects=True, vmem_limit_bytes=VMEM_LIMIT),
    )(terms, density)


def on_device(orb_blocks, pno, pno_levels, occ_levels, pair_i_local, fetch_local, pair_slot):
    n = lax.axis_size("orb")
    orbs = orb_blocks.shape[0]
    pairs = pno.shape[0]
    slots = fetch_local.shape[0]
    orb_total = orbs * n
    per_owner = slots // n
    slot_of = pair_slot[:, 0]
    slot_ids = jnp.arange(slots, dtype=jnp.int32)
    pair_ids = jnp.arange(pairs, dtype=jnp.int32)
    slot_orb = slot_ids // per_owner * orbs + fetch_local
    first_glob = lax.axis_index("orb") * orbs + pair_i_local
    second = jnp.sum(jnp.where(slot_of[:, None] == slot_ids[None, :], slot_orb[None, :], 0), axis=1)
    same = slot_of[:, None] == slot_of[None, :]
    fresh = 1 - jnp.any(same & (pair_ids[None, :] < pair_ids[:, None]), axis=1).astype(jnp.int32)
    final = 1 - jnp.any(same & (pair_ids[None, :] > pair_ids[:, None]), axis=1).astype(jnp.int32)
    seen = jnp.any(second[:, None] == jnp.arange(orb_total, dtype=jnp.int32)[None, :], axis=0).astype(jnp.int32)
    info = jnp.pad(occ_levels[None, :], ((0, 7), (0, 128 - orbs)))
    rank = jnp.sum((same & (pair_ids[None, :] < pair_ids[:, None])).astype(jnp.int32), axis=1)
    row_of = slot_of * MOST + rank
    row_ids = jnp.arange(slots * MOST, dtype=jnp.int32)
    row_pair = jnp.max(jnp.where(row_of[None, :] == row_ids[:, None], pair_ids[None, :], -1), axis=1)
    fp, sp, coulomb, energies, info_all = gather(
        n, pair_i_local, fetch_local, row_pair, orb_blocks, pno, pno_levels, info
    )
    info_all = info_all[:, 0, :orbs]
    shifts = shift_call(n, orb_total, energies)
    scalars = (pair_i_local, slot_of, second, first_glob, fresh, final, seen, row_of)
    amplitude, density, terms = density_call(
        scalars, info_all, shifts, orbs, slots, orb_total, pno, pno_levels, fp, sp, coulomb
    )
    return (amplitude, home(n, terms, density))


def solution(mesh):
    placed = (
        P(("image", "orb"), None, None),
        P(("image", "orb"), None, None),
        P(("image", "orb"), None),
        P(("image", "orb")),
        P(("image", "orb")),
        P(("image", "orb")),
        P(("image", "orb"), None),
    )
    return jax.shard_map(
        on_device,
        mesh=mesh,
        in_specs=placed,
        out_specs=(P(("image", "orb"), None, None), P(("image", "orb"), None, None)),
        check_vma=False,
    )
```

```python
import functools

import jax
import jax.numpy as jnp
from jax import lax
from jax.experimental import pallas as pl
from jax.experimental.pallas import tpu as pltpu
from jax.sharding import PartitionSpec as P

MOST = 3
ITERS = 2
shift_weight = 0.1
MESH = pl.DeviceIdType.MESH
F32 = jnp.float32
BF16 = jnp.bfloat16
VMEM_LIMIT = 56 * 1024 * 1024


def chip_at(position, chips):
    position = lax.rem(position + 2 * chips, chips)
    if chips == 8:
        far = position // 4
        return 2 * (position + far * (7 - 2 * position)) + far
    return position


def place_of(chip, chips):
    if chips == 8:
        y = lax.rem(chip, 2)
        z = chip // 2
        return z + y * (7 - 2 * z)
    return chip


def ring(n):
    me = lax.axis_index("orb")
    chips = n // 2
    core = lax.rem(me, 2)
    place = place_of(me // 2, chips)

    def dev(position, c):
        return chip_at(position, chips) * 2 + c

    return me, chips, core, place, dev


def greet(others):
    barrier = pltpu.get_barrier_semaphore()
    for other in others:
        pl.semaphore_signal(barrier, inc=1, device_id={"orb": other}, device_id_type=MESH)
    pl.semaphore_wait(barrier, len(others))


def remote(src, dst, send, recv, target):
    return pltpu.make_async_remote_copy(
        src_ref=src, dst_ref=dst, send_sem=send, recv_sem=recv, device_id={"orb": target}, device_id_type=MESH
    )


def gather_kernel(n, per_owner, first_s, fetch_s, row_s, x_ref, pno_ref, level_ref, info_ref,
                  fp_out, sp_out, c_out, e_ref, info_out,
                  blocks, moments, fp_stage, sp_stage, c_stage,
                  own_sem, first_send, first_recv, ring_send, ring_recv, side_send, side_recv, info_send, info_recv, out_sem):
    me, chips, core, place, dev = ring(n)
    orbs = x_ref.shape[0]
    half = orbs // 2
    width = pno_ref.shape[1]
    rows = per_owner * MOST
    scale = x_ref.shape[2] ** -0.5
    norm = -1.0 / (width * width)
    sibling = me + 1 - 2 * core
    ends = (dev(place + 1, core), dev(place - 1, core))
    lane = lax.broadcasted_iota(jnp.int32, (1, 128), 1)
    greet([lax.rem(me + d, n) for d in range(1, n)])

    def owner_at(way, step):
        return dev(place - step if way == 0 else place + step, way)

    def first_copy(k):
        local = lax.rem(half * (1 - core) + k, orbs)
        return remote(x_ref.at[local], blocks.at[me, local], first_send.at[k], first_recv.at[k], sibling)

    def ring_copy(way, step, k):
        block = blocks.at[owner_at(way, step - 1), half * core + k]
        return remote(block, block, ring_send.at[way, step, k], ring_recv.at[way, step, k], ends[way])

    def ring_wait(way, step, k):
        block = blocks.at[owner_at(way, step), half * core + k]
        remote(block, block, ring_send.at[way, step, k], ring_recv.at[way, step, k], ends[way]).wait_recv()

    def side_copy(way, step, k):
        block = blocks.at[owner_at(way, step), half * core + k]
        return remote(block, block, side_send.at[way, step, k], side_recv.at[way, step, k], sibling)

    def side_wait(way, step, k):
        block = blocks.at[owner_at(way, step), half * (1 - core) + k]
        remote(block, block, side_send.at[way, step, k], side_recv.at[way, step, k], sibling).wait_recv()

    def note(d):
        return remote(info_ref, info_out.at[me], info_send.at[d - 1], info_recv.at[d - 1], lax.rem(me + d, n))

    def out_copies(way, owner, i):
        row = owner * rows + i
        return [
            pltpu.make_async_copy(stage.at[way, i], out.at[row], out_sem.at[way, kind, i])
            for kind, (stage, out) in enumerate(((fp_stage, fp_out), (sp_stage, sp_out), (c_stage, c_out)))
        ]

    def work(way, step):
        owner = owner_at(way, step)
        for s in range(per_owner):
            local = fetch_s[owner * per_owner + s]
            block = blocks[owner, 0]
            for other in range(1, orbs):
                block = jnp.where(local == other, blocks[owner, other], block)
            occ2 = jnp.sum(jnp.where(lane == local, info_out[owner, 0:1, :], 0.0), axis=1, keepdims=True)
            base = owner * rows + s * MOST
            named = [row_s[base + m] for m in range(MOST)]
            pair = [jnp.maximum(q, 0) for q in named]
            first = [first_s[q] for q in pair]
            w = [pno_ref[q] for q in pair]
            inverse = []
            for m in range(MOST):
                levels = jnp.broadcast_to(level_ref[pair[m]], (width, width))
                occ1 = jnp.sum(jnp.where(lane == first[m], info_ref[0:1, :], 0.0), axis=1, keepdims=True)
                inverse.append(1.0 / (levels + levels.T - (occ1 + occ2)))
            sp = [jnp.dot(w[m], block, preferred_element_type=F32).astype(BF16) for m in range(MOST)]
            fp = [jnp.dot(w[m], x_ref[first[m]], preferred_element_type=F32).astype(BF16) for m in range(MOST)]
            c = [
                lax.dot_general(fp[m], sp[m], (((1,), (1,)), ((), ())), preferred_element_type=F32) * scale
                for m in range(MOST)
            ]
            t = [c[m] * (2.0 * c[m] - c[m].T) * inverse[m] for m in range(MOST)]
            for m in range(MOST):
                i = s * MOST + m
                fp_stage[way, i] = fp[m]
                sp_stage[way, i] = sp[m]
                c_stage[way, i] = c[m]
                moments[0, pl.ds(base + m, 1), :] = jnp.sum(t[m], axis=0, keepdims=True)
                moments[1, pl.ds(base + m, 1), :] = jnp.sum(t[m] * inverse[m], axis=0, keepdims=True)
                here = lane == base + m
                id1 = jnp.where(named[m] >= 0, me * orbs + first[m], -1).astype(F32)
                id2 = jnp.where(named[m] >= 0, owner * orbs + local, -1).astype(F32)
                e_ref[2:3, :] = jnp.where(here, id1, e_ref[2:3, :])
                e_ref[3:4, :] = jnp.where(here, id2, e_ref[3:4, :])
        for i in range(rows):
            for copy in out_copies(way, owner, i):
                copy.start()

    for k in range(orbs):
        first_copy(k).start()
    own = pltpu.make_async_copy(x_ref, blocks.at[me], own_sem.at[0])
    own.start()
    own.wait()
    for k in range(half):
        first_copy(k).wait_recv()
    for k in range(half):
        for way in range(2):
            ring_copy(way, 1, k).start()
    for d in range(1, n):
        note(d).start()
    info_out[me] = info_ref[...]
    e_ref[...] = jnp.zeros_like(e_ref)
    e_ref[2:4, :] = jnp.full((2, 128), -1.0, F32)
    moments[...] = jnp.zeros_like(moments)
    for k in range(half, orbs):
        first_copy(k).wait_recv()
    for d in range(1, n):
        note(d).wait()

    def turn(step, carry):
        for k in range(half):
            @pl.when(step < chips)
            def _():
                for way in range(2):
                    ring_wait(way, step, k)

                    @pl.when(step < chips - 1)
                    def _():
                        ring_copy(way, step + 1, k).start()

                    side_copy(way, step, k).start()

            for way in range(2):
                if way % half == k:
                    @pl.when(step > 1)
                    def _():
                        for kk in range(half):
                            side_wait(way, step - 1, kk)
                        for i in range(rows):
                            for copy in out_copies(way, owner_at(way, step - 2), i):
                                copy.wait()

                    work(way, step - 1)
        return carry

    lax.fori_loop(1, chips + 1, turn, 0)
    square = lax.broadcasted_iota(jnp.int32, (128, 128), 0) == lax.broadcasted_iota(jnp.int32, (128, 128), 1)
    for kind in range(2):
        column = jnp.sum(moments[kind], axis=1, keepdims=True) * norm
        e_ref[kind:kind + 1, :] = jnp.sum(jnp.where(square, column, 0.0), axis=0, keepdims=True)
    for way in range(2):
        for i in range(rows):
            for copy in out_copies(way, owner_at(way, chips - 1), i):
                copy.wait()
    for k in range(orbs):
        first_copy(k).wait_send()

    def drain(step, carry):
        for k in range(half):
            for way in range(2):
                ring_copy(way, step, k).wait_send()
                side_copy(way, step, k).wait_send()
        return carry

    lax.fori_loop(1, chips, drain, 0)


def gather(n, first_local, fetch_local, row_pair, x, pno, levels, info):
    pairs, width, nvirt = pno.shape
    orbs, _, aux = x.shape
    per_owner = fetch_local.shape[0] // n
    rows = per_owner * MOST
    total = rows * n
    chips, half = n // 2, orbs // 2
    dma = pltpu.SemaphoreType.DMA
    smem, vmem, anywhere = (pl.BlockSpec(memory_space=m) for m in (pltpu.SMEM, pltpu.VMEM, pl.ANY))
    return pl.pallas_call(
        functools.partial(gather_kernel, n, per_owner),
        name="gather_coulomb",
        out_shape=(
            jax.ShapeDtypeStruct((total, width, aux), BF16),
            jax.ShapeDtypeStruct((total, width, aux), BF16),
            jax.ShapeDtypeStruct((total, width, width), F32),
            jax.ShapeDtypeStruct((8, 128), F32),
            jax.ShapeDtypeStruct((n,) + info.shape, info.dtype),
        ),
        in_specs=[smem, smem, smem, vmem, vmem, vmem, vmem],
        out_specs=(anywhere, anywhere, anywhere, vmem, vmem),
        scratch_shapes=[
            pltpu.VMEM((n, orbs, nvirt, aux), BF16),
            pltpu.VMEM((2, 128, width), F32),
            pltpu.VMEM((2, rows, width, aux), BF16),
            pltpu.VMEM((2, rows, width, aux), BF16),
            pltpu.VMEM((2, rows, width, width), F32),
            dma((1,)), dma((orbs,)), dma((orbs,)),
            dma((2, chips, half)), dma((2, chips, half)), dma((2, chips, half)), dma((2, chips, half)),
            dma((n - 1,)), dma((n - 1,)), dma((2, 3, rows)),
        ],
        compiler_params=pltpu.CompilerParams(collective_id=0, has_side_effects=True, vmem_limit_bytes=VMEM_LIMIT),
    )(first_local, fetch_local, row_pair, x, pno, levels.reshape(pairs, 1, width), info)


def group_of(pairs):
    return next(g for g in (4, 3, 2, 1) if pairs % g == 0)


def shift_kernel(n, orb_total, e_ref, out_ref, got, send, recv):
    me = lax.axis_index("orb")
    greet([lax.rem(me + d, n) for d in range(1, n)])
    copies = []
    for d in range(1, n):
        copy = remote(e_ref, got.at[me], send.at[d - 1], recv.at[d - 1], lax.rem(me + d, n))
        copy.start()
        copies.append(copy)
    got[me] = e_ref[...]
    for copy in copies:
        copy.wait()
    ids = lax.broadcasted_iota(jnp.int32, (orb_total, 128), 0).astype(F32)

    def shares(block):
        return jnp.where(ids == block[2:3, :], 1.0, 0.0) + jnp.where(ids == block[3:4, :], 1.0, 0.0)

    total = jnp.zeros((orb_total, 128), F32)
    for d in range(n):
        block = got[d]
        total = total + shares(block) * block[0:1, :]
    shift = shift_weight * jnp.sum(total, axis=1, keepdims=True)
    total = jnp.zeros((orb_total, 128), F32)
    for d in range(n):
        block = got[d]
        hot = shares(block)
        pair_shift = jnp.sum(hot * shift, axis=0, keepdims=True)
        total = total + hot * (block[0:1, :] - pair_shift * block[1:2, :])
    shift2 = shift_weight * jnp.sum(total, axis=1, keepdims=True)
    mine = shares(e_ref[...])
    out_ref[...] = jnp.zeros_like(out_ref)
    out_ref[0:1, :] = jnp.sum(mine * shift, axis=0, keepdims=True)
    out_ref[1:2, :] = jnp.sum(mine * shift2, axis=0, keepdims=True)


def shift_call(n, orb_total, energies):
    dma = pltpu.SemaphoreType.DMA
    return pl.pallas_call(
        functools.partial(shift_kernel, n, orb_total),
        name="shifts",
        out_shape=jax.ShapeDtypeStruct((8, 128), F32),
        in_specs=[pl.BlockSpec(memory_space=pltpu.VMEM)],
        out_specs=pl.BlockSpec(memory_space=pltpu.VMEM),
        scratch_shapes=[pltpu.VMEM((n, 8, 128), F32), dma((n - 1,)), dma((n - 1,))],
        compiler_params=pltpu.CompilerParams(collective_id=1, has_side_effects=True, vmem_limit_bytes=VMEM_LIMIT),
    )(energies)


def density_kernel(group, orbs, first_s, slot_s, second_s, fglob_s, fresh_s, final_s, seen_s, row_s,
                   info_s, shift_s, pno_ref, level_ref, *rest):
    fp_refs, sp_refs, c_refs = rest[:group], rest[group:2 * group], rest[2 * group:3 * group]
    amp_ref, dens_ref, terms_ref, acc, stage, blank, busy, stage_sem, blank_sem = rest[3 * group:]
    step = pl.program_id(0)
    width = pno_ref.shape[1]
    aux = fp_refs[0].shape[2]
    total = terms_ref.shape[0]

    def blank_copy(o):
        return pltpu.make_async_copy(blank, terms_ref.at[o], blank_sem.at[0])

    @pl.when(step == 0)
    def _():
        dens_ref[...] = jnp.zeros_like(dens_ref)
        blank[...] = jnp.zeros_like(blank)
        for j in range(group):
            busy[j] = 0

        @pl.loop(0, total)
        def _(o):
            @pl.when(seen_s[o] == 0)
            def _():
                blank_copy(o).start()

    halves = []
    for j in range(group):
        p = step * group + j
        fg, sg = fglob_s[p], second_s[p]
        levels = jnp.broadcast_to(level_ref[0, j:j + 1, :], (width, width))
        occ = info_s[fg // orbs, lax.rem(fg, orbs)] + info_s[sg // orbs, lax.rem(sg, orbs)]
        inverse = 1.0 / (levels + levels.T - occ)
        s1, s2 = shift_s[0, row_s[p]], shift_s[1, row_s[p]]
        amp = -c_refs[j][0] * inverse * (1.0 - s2 * inverse * (1.0 - s1 * inverse))
        amp_ref[j] = amp
        halves.append(amp.astype(BF16))
    parts = []
    for j in range(group):
        part1 = jnp.dot(halves[j], sp_refs[j][0], preferred_element_type=F32).astype(BF16)
        part2 = lax.dot_general(halves[j], fp_refs[j][0], (((0,), (0,)), ((), ())), preferred_element_type=F32).astype(BF16)
        parts.append(jnp.concatenate([part1, part2], axis=1))
    for j in range(group):
        p = step * group + j
        slot = slot_s[p]
        pao = lax.dot_general(pno_ref[j], parts[j], (((0,), (0,)), ((), ())), preferred_element_type=F32)
        dens_ref[first_s[p]] += pao[:, :aux]
        term = pao[:, aux:]
        acc[slot] = jnp.where(fresh_s[p] == 1, term, acc[slot] + term)

    for j in range(group):
        p = step * group + j
        sg, slot = second_s[p], slot_s[p]

        @pl.when(final_s[p] == 1)
        def _():
            copy = pltpu.make_async_copy(stage.at[j], terms_ref.at[sg], stage_sem.at[j])

            @pl.when(busy[j] == 1)
            def _():
                copy.wait()

            stage[j] = acc[slot].astype(BF16)
            copy.start()
            busy[j] = 1

    @pl.when(step == pl.num_programs(0) - 1)
    def _():
        for j in range(group):
            @pl.when(busy[j] == 1)
            def _():
                pltpu.make_async_copy(stage.at[j], terms_ref.at[0], stage_sem.at[j]).wait()

        @pl.loop(0, total)
        def _(o):
            @pl.when(seen_s[o] == 0)
            def _():
                blank_copy(o).wait()


def density_call(scalars, info, shifts, orbs, slots, orb_total, pno, levels, fp, sp, c):
    pairs, width, nvirt = pno.shape
    aux = fp.shape[2]
    group = group_of(pairs)
    three = lambda i, *_: (i, 0, 0)

    def row_map(j, i, *scalars):
        return (scalars[-1][i * group + j], 0, 0)

    def picked(array):
        return [pl.BlockSpec((1,) + array.shape[1:], functools.partial(row_map, j)) for j in range(group)]

    smem = pl.BlockSpec(memory_space=pltpu.SMEM)
    dma = pltpu.SemaphoreType.DMA
    return pl.pallas_call(
        functools.partial(density_kernel, group, orbs),
        name="density_terms",
        out_shape=(
            jax.ShapeDtypeStruct((pairs, width, width), F32),
            jax.ShapeDtypeStruct((orbs, nvirt, aux), F32),
            jax.ShapeDtypeStruct((orb_total, nvirt, aux), BF16),
        ),
        grid_spec=pltpu.PrefetchScalarGridSpec(
            num_scalar_prefetch=8,
            grid=(pairs // group,),
            in_specs=[
                smem, smem,
                pl.BlockSpec((group, width, nvirt), three),
                pl.BlockSpec((1, group, width), three),
            ] + picked(fp) + picked(sp) + picked(c),
            out_specs=(
                pl.BlockSpec((group, width, width), three),
                pl.BlockSpec((orbs, nvirt, aux), lambda i, *_: (0, 0, 0)),
                pl.BlockSpec(memory_space=pl.ANY),
            ),
            scratch_shapes=[
                pltpu.VMEM((slots, nvirt, aux), F32),
                pltpu.VMEM((group, nvirt, aux), BF16),
                pltpu.VMEM((nvirt, aux), BF16),
                pltpu.SMEM((group,), jnp.int32),
                dma((group,)), dma((1,)),
            ],
        ),
        compiler_params=pltpu.CompilerParams(vmem_limit_bytes=VMEM_LIMIT),
    )(*scalars, info, shifts, pno, levels.reshape(pairs // group, group, width), *([fp] * group + [sp] * group + [c] * group))


def home_kernel(n, terms_ref, dens_ref, out_ref, own, side, got, own_sem, side_send, side_recv, ring_send, ring_recv):
    me, chips, core, place, dev = ring(n)
    orbs, rows = dens_ref.shape[0], dens_ref.shape[1]
    half = orbs // 2
    sibling = me + 1 - 2 * core
    ends = (dev(place + 1, core), dev(place - 1, core))
    greet([ends[0], ends[1], sibling])
    chunk = 32

    def position(way, step):
        return place - 1 - step if way == 0 else place + 1 + step

    def own_copy(way, step, k):
        r = dev(position(way, step), core) * orbs + way * half + k
        return pltpu.make_async_copy(terms_ref.at[r], own.at[way, step, k], own_sem.at[way, step, k])

    def side_copy(way, step, k):
        r = dev(position(way, step), 1 - core) * orbs + way * half + k
        return remote(terms_ref.at[r], side.at[way, step, k], side_send.at[way, step, k], side_recv.at[way, step, k], sibling)

    def load(step):
        for k in range(half):
            for way in range(2):
                side_copy(way, step, k).start()
                own_copy(way, step, k).start()

    def ring_copy(way, step, k):
        return remote(side.at[way, step, k], got.at[way, step, k], ring_send.at[way, step, k], ring_recv.at[way, step, k], ends[way])

    load(0)
    load(1)
    for step in range(chips):
        for k in range(half):
            for way in range(2):
                own_copy(way, step, k).wait()
                side_copy(way, step, k).wait_recv()
                if step > 0:
                    ring_copy(way, step - 1, k).wait_recv()

                @pl.loop(0, rows // chunk)
                def _(i):
                    at = pl.ds(pl.multiple_of(i * chunk, chunk), chunk)
                    total = own[way, step, k, at, :].astype(F32) + side[way, step, k, at, :].astype(F32)
                    if step > 0:
                        total = total + got[way, step - 1, k, at, :].astype(F32)
                    if step < chips - 1:
                        side[way, step, k, at, :] = total.astype(BF16)
                    else:
                        out_ref[way * half + k, at, :] = dens_ref[way * half + k, at, :] + total

                if step < chips - 1:
                    ring_copy(way, step, k).start()
        if step + 2 < chips:
            load(step + 2)
    for step in range(chips):
        for k in range(half):
            for way in range(2):
                side_copy(way, step, k).wait_send()
                if step < chips - 1:
                    ring_copy(way, step, k).wait_send()


def home(n, terms, density):
    orbs, nvirt, aux = density.shape
    chips, half = n // 2, orbs // 2
    dma = pltpu.SemaphoreType.DMA
    many = (2, chips, half)
    return pl.pallas_call(
        functools.partial(home_kernel, n),
        name="terms_home",
        out_shape=jax.ShapeDtypeStruct(density.shape, F32),
        in_specs=[pl.BlockSpec(memory_space=pl.ANY), pl.BlockSpec(memory_space=pltpu.VMEM)],
        out_specs=pl.BlockSpec(memory_space=pltpu.VMEM),
        scratch_shapes=[
            pltpu.VMEM(many + (nvirt, aux), BF16),
            pltpu.VMEM(many + (nvirt, aux), BF16),
            pltpu.VMEM((2, chips - 1, half, nvirt, aux), BF16),
            dma(many), dma(many), dma(many), dma(many), dma(many),
        ],
        compiler_params=pltpu.CompilerParams(collective_id=2, has_side_effects=True, vmem_limit_bytes=VMEM_LIMIT),
    )(terms, density)


def on_device(orb_blocks, pno, pno_levels, occ_levels, pair_i_local, fetch_local, pair_slot):
    n = lax.axis_size("orb")
    orbs = orb_blocks.shape[0]
    pairs = pno.shape[0]
    slots = fetch_local.shape[0]
    orb_total = orbs * n
    per_owner = slots // n
    slot_of = pair_slot[:, 0]
    slot_ids = jnp.arange(slots, dtype=jnp.int32)
    pair_ids = jnp.arange(pairs, dtype=jnp.int32)
    slot_orb = slot_ids // per_owner * orbs + fetch_local
    first_glob = lax.axis_index("orb") * orbs + pair_i_local
    second = jnp.sum(jnp.where(slot_of[:, None] == slot_ids[None, :], slot_orb[None, :], 0), axis=1)
    same = slot_of[:, None] == slot_of[None, :]
    fresh = 1 - jnp.any(same & (pair_ids[None, :] < pair_ids[:, None]), axis=1).astype(jnp.int32)
    final = 1 - jnp.any(same & (pair_ids[None, :] > pair_ids[:, None]), axis=1).astype(jnp.int32)
    seen = jnp.any(second[:, None] == jnp.arange(orb_total, dtype=jnp.int32)[None, :], axis=0).astype(jnp.int32)
    info = jnp.pad(occ_levels[None, :], ((0, 7), (0, 128 - orbs)))
    rank = jnp.sum((same & (pair_ids[None, :] < pair_ids[:, None])).astype(jnp.int32), axis=1)
    row_of = slot_of * MOST + rank
    row_ids = jnp.arange(slots * MOST, dtype=jnp.int32)
    row_pair = jnp.max(jnp.where(row_of[None, :] == row_ids[:, None], pair_ids[None, :], -1), axis=1)
    fp, sp, coulomb, energies, info_all = gather(
        n, pair_i_local, fetch_local, row_pair, orb_blocks, pno, pno_levels, info
    )
    info_all = info_all[:, 0, :orbs]
    shifts = shift_call(n, orb_total, energies)
    scalars = (pair_i_local, slot_of, second, first_glob, fresh, final, seen, row_of)
    amplitude, density, terms = density_call(
        scalars, info_all, shifts, orbs, slots, orb_total, pno, pno_levels, fp, sp, coulomb
    )
    return (amplitude, home(n, terms, density))


def solution(mesh):
    placed = (
        P(("image", "orb"), None, None),
        P(("image", "orb"), None, None),
        P(("image", "orb"), None),
        P(("image", "orb")),
        P(("image", "orb")),
        P(("image", "orb")),
        P(("image", "orb"), None),
    )
    return jax.shard_map(
        on_device,
        mesh=mesh,
        in_specs=placed,
        out_specs=(P(("image", "orb"), None, None), P(("image", "orb"), None, None)),
        check_vma=False,
    )
```

```python
import functools

import jax
import jax.numpy as jnp
from jax import lax
from jax.experimental import pallas as pl
from jax.experimental.pallas import tpu as pltpu
from jax.sharding import PartitionSpec as P

MOST = 3
ITERS = 2
shift_weight = 0.1
MESH = pl.DeviceIdType.MESH
F32 = jnp.float32
BF16 = jnp.bfloat16
VMEM_LIMIT = 56 * 1024 * 1024


def chip_at(position, chips):
    position = lax.rem(position + 2 * chips, chips)
    if chips == 8:
        far = position // 4
        return 2 * (position + far * (7 - 2 * position)) + far
    return position


def place_of(chip, chips):
    if chips == 8:
        y = lax.rem(chip, 2)
        z = chip // 2
        return z + y * (7 - 2 * z)
    return chip


def ring(n):
    me = lax.axis_index("orb")
    chips = n // 2
    core = lax.rem(me, 2)
    place = place_of(me // 2, chips)

    def dev(position, c):
        return chip_at(position, chips) * 2 + c

    return me, chips, core, place, dev


def greet(others):
    barrier = pltpu.get_barrier_semaphore()
    for other in others:
        pl.semaphore_signal(barrier, inc=1, device_id={"orb": other}, device_id_type=MESH)
    pl.semaphore_wait(barrier, len(others))


def remote(src, dst, send, recv, target):
    return pltpu.make_async_remote_copy(
        src_ref=src, dst_ref=dst, send_sem=send, recv_sem=recv, device_id={"orb": target}, device_id_type=MESH
    )


def shifts(n, orb_total, e_ref, got, out_ref):
    ids = lax.broadcasted_iota(jnp.int32, (orb_total, 128), 0).astype(F32)

    def shares(block):
        return jnp.where(ids == block[2:3, :], 1.0, 0.0) + jnp.where(ids == block[3:4, :], 1.0, 0.0)

    total = jnp.zeros((orb_total, 128), F32)
    for d in range(n):
        block = got[d]
        total = total + shares(block) * block[0:1, :]
    shift = shift_weight * jnp.sum(total, axis=1, keepdims=True)
    total = jnp.zeros((orb_total, 128), F32)
    for d in range(n):
        block = got[d]
        hot = shares(block)
        pair_shift = jnp.sum(hot * shift, axis=0, keepdims=True)
        total = total + hot * (block[0:1, :] - pair_shift * block[1:2, :])
    shift2 = shift_weight * jnp.sum(total, axis=1, keepdims=True)
    mine = shares(e_ref[...])
    out_ref[...] = jnp.zeros_like(out_ref)
    out_ref[0:1, :] = jnp.sum(mine * shift, axis=0, keepdims=True)
    out_ref[1:2, :] = jnp.sum(mine * shift2, axis=0, keepdims=True)
    out_ref[2:3, :] = e_ref[4:5, :]


def gather_kernel(n, per_owner, first_s, fetch_s, row_s, occ_s, x_ref, pno_in, level_ref,
                  fp_out, sp_out, c_out, shift_ref,
                  pno_ref, info_ref, info_out, e_ref, got, blocks, moments, fp_stage, sp_stage, c_stage,
                  own_sem, first_send, first_recv, ring_send, ring_recv, side_send, side_recv, info_send, info_recv, e_send, e_recv, out_sem):
    me, chips, core, place, dev = ring(n)
    orbs = x_ref.shape[0]
    half = orbs // 2
    width = pno_ref.shape[1]
    rows = per_owner * MOST
    scale = x_ref.shape[2] ** -0.5
    norm = -1.0 / (width * width)
    sibling = me + 1 - 2 * core
    ends = (dev(place + 1, core), dev(place - 1, core))
    lane = lax.broadcasted_iota(jnp.int32, (1, 128), 1)
    pno_copy = pltpu.make_async_copy(pno_in, pno_ref, own_sem.at[1])
    pno_copy.start()
    levels_row = jnp.zeros((8, 128), F32)
    for l in range(orbs):
        levels_row = jnp.where(lane == l, occ_s[l], levels_row)
    info_ref[...] = levels_row
    greet([lax.rem(me + d, n) for d in range(1, n)])

    def owner_at(way, step):
        return dev(place - step if way == 0 else place + step, way)

    def first_copy(k):
        local = lax.rem(half * (1 - core) + k, orbs)
        return remote(x_ref.at[local], blocks.at[me, local], first_send.at[k], first_recv.at[k], sibling)

    def ring_copy(way, step, k):
        block = blocks.at[owner_at(way, step - 1), half * core + k]
        return remote(block, block, ring_send.at[way, step, k], ring_recv.at[way, step, k], ends[way])

    def ring_wait(way, step, k):
        block = blocks.at[owner_at(way, step), half * core + k]
        remote(block, block, ring_send.at[way, step, k], ring_recv.at[way, step, k], ends[way]).wait_recv()

    def side_copy(way, step, k):
        block = blocks.at[owner_at(way, step), half * core + k]
        return remote(block, block, side_send.at[way, step, k], side_recv.at[way, step, k], sibling)

    def side_wait(way, step, k):
        block = blocks.at[owner_at(way, step), half * (1 - core) + k]
        remote(block, block, side_send.at[way, step, k], side_recv.at[way, step, k], sibling).wait_recv()

    def note(d):
        return remote(info_ref, info_out.at[me], info_send.at[d - 1], info_recv.at[d - 1], lax.rem(me + d, n))

    def out_copies(way, owner, i):
        row = owner * rows + i
        return [
            pltpu.make_async_copy(stage.at[way, i], out.at[row], out_sem.at[way, kind, i])
            for kind, (stage, out) in enumerate(((fp_stage, fp_out), (sp_stage, sp_out), (c_stage, c_out)))
        ]

    def work(way, step):
        owner = owner_at(way, step)
        for s in range(per_owner):
            local = fetch_s[owner * per_owner + s]
            block = blocks[owner, 0]
            for other in range(1, orbs):
                block = jnp.where(local == other, blocks[owner, other], block)
            occ2 = jnp.sum(jnp.where(lane == local, info_out[owner, 0:1, :], 0.0), axis=1, keepdims=True)
            base = owner * rows + s * MOST
            named = [row_s[base + m] for m in range(MOST)]
            pair = [jnp.maximum(q, 0) for q in named]
            first = [first_s[q] for q in pair]
            w = [pno_ref[q] for q in pair]
            inverse, occ = [], []
            for m in range(MOST):
                levels = jnp.broadcast_to(level_ref[pl.ds(pair[m], 1), :], (width, width))
                occ1 = jnp.sum(jnp.where(lane == first[m], info_ref[0:1, :], 0.0), axis=1, keepdims=True)
                occ.append(occ1 + occ2)
                inverse.append(1.0 / (levels + levels.T - occ[m]))
            sp = [jnp.dot(w[m], block, preferred_element_type=F32).astype(BF16) for m in range(MOST)]
            fp = [jnp.dot(w[m], x_ref[first[m]], preferred_element_type=F32).astype(BF16) for m in range(MOST)]
            c = [
                lax.dot_general(fp[m], sp[m], (((1,), (1,)), ((), ())), preferred_element_type=F32) * scale
                for m in range(MOST)
            ]
            t = [c[m] * (2.0 * c[m] - c[m].T) * inverse[m] for m in range(MOST)]
            for m in range(MOST):
                i = s * MOST + m
                fp_stage[way, i] = fp[m]
                sp_stage[way, i] = sp[m]
                c_stage[way, i] = c[m]
                moments[0, pl.ds(base + m, 1), :] = jnp.sum(t[m], axis=0, keepdims=True)
                moments[1, pl.ds(base + m, 1), :] = jnp.sum(t[m] * inverse[m], axis=0, keepdims=True)
                here = lane == base + m
                id1 = jnp.where(named[m] >= 0, me * orbs + first[m], -1).astype(F32)
                id2 = jnp.where(named[m] >= 0, owner * orbs + local, -1).astype(F32)
                e_ref[2:3, :] = jnp.where(here, id1, e_ref[2:3, :])
                e_ref[3:4, :] = jnp.where(here, id2, e_ref[3:4, :])
                e_ref[4:5, :] = jnp.where(here, occ[m], e_ref[4:5, :])
        for i in range(rows):
            for copy in out_copies(way, owner, i):
                copy.start()

    for k in range(orbs):
        first_copy(k).start()
    own = pltpu.make_async_copy(x_ref, blocks.at[me], own_sem.at[0])
    own.start()
    own.wait()
    for k in range(half):
        first_copy(k).wait_recv()
    for k in range(half):
        for way in range(2):
            ring_copy(way, 1, k).start()
    for d in range(1, n):
        note(d).start()
    info_out[me] = info_ref[...]
    e_ref[...] = jnp.zeros_like(e_ref)
    e_ref[2:4, :] = jnp.full((2, 128), -1.0, F32)
    moments[...] = jnp.zeros_like(moments)
    for k in range(half, orbs):
        first_copy(k).wait_recv()
    for d in range(1, n):
        note(d).wait()
    pno_copy.wait()

    def turn(step, carry):
        for k in range(half):
            @pl.when(step < chips)
            def _():
                for way in range(2):
                    ring_wait(way, step, k)

                    @pl.when(step < chips - 1)
                    def _():
                        ring_copy(way, step + 1, k).start()

                    side_copy(way, step, k).start()

            for way in range(2):
                if way % half == k:
                    @pl.when(step > 1)
                    def _():
                        for kk in range(half):
                            side_wait(way, step - 1, kk)
                        for i in range(rows):
                            for copy in out_copies(way, owner_at(way, step - 2), i):
                                copy.wait()

                    work(way, step - 1)
        return carry

    lax.fori_loop(1, chips + 1, turn, 0)
    square = lax.broadcasted_iota(jnp.int32, (128, 128), 0) == lax.broadcasted_iota(jnp.int32, (128, 128), 1)
    for kind in range(2):
        column = jnp.sum(moments[kind], axis=1, keepdims=True) * norm
        e_ref[kind:kind + 1, :] = jnp.sum(jnp.where(square, column, 0.0), axis=0, keepdims=True)

    def energy_copy(d):
        return remote(e_ref, got.at[me], e_send.at[d - 1], e_recv.at[d - 1], lax.rem(me + d, n))

    for d in range(1, n):
        energy_copy(d).start()
    got[me] = e_ref[...]
    for d in range(1, n):
        energy_copy(d).wait()
    shifts(n, n * orbs, e_ref, got, shift_ref)
    for way in range(2):
        for i in range(rows):
            for copy in out_copies(way, owner_at(way, chips - 1), i):
                copy.wait()
    for k in range(orbs):
        first_copy(k).wait_send()

    def drain(step, carry):
        for k in range(half):
            for way in range(2):
                ring_copy(way, step, k).wait_send()
                side_copy(way, step, k).wait_send()
        return carry

    lax.fori_loop(1, chips, drain, 0)


def gather(n, first_local, fetch_local, row_pair, occ, x, pno, levels):
    pairs, width, nvirt = pno.shape
    orbs, _, aux = x.shape
    per_owner = fetch_local.shape[0] // n
    rows = per_owner * MOST
    total = rows * n
    chips, half = n // 2, orbs // 2
    dma = pltpu.SemaphoreType.DMA
    smem, vmem, anywhere = (pl.BlockSpec(memory_space=m) for m in (pltpu.SMEM, pltpu.VMEM, pl.ANY))
    return pl.pallas_call(
        functools.partial(gather_kernel, n, per_owner),
        name="gather_coulomb",
        out_shape=(
            jax.ShapeDtypeStruct((total, width, aux), BF16),
            jax.ShapeDtypeStruct((total, width, aux), BF16),
            jax.ShapeDtypeStruct((total, width, width), F32),
            jax.ShapeDtypeStruct((8, 128), F32),
        ),
        in_specs=[smem, smem, smem, smem, vmem, anywhere, vmem],
        out_specs=(anywhere, anywhere, anywhere, vmem),
        scratch_shapes=[
            pltpu.VMEM(pno.shape, BF16),
            pltpu.VMEM((8, 128), F32),
            pltpu.VMEM((n, 8, 128), F32),
            pltpu.VMEM((8, 128), F32),
            pltpu.VMEM((n, 8, 128), F32),
            pltpu.VMEM((n, orbs, nvirt, aux), BF16),
            pltpu.VMEM((2, 128, width), F32),
            pltpu.VMEM((2, rows, width, aux), BF16),
            pltpu.VMEM((2, rows, width, aux), BF16),
            pltpu.VMEM((2, rows, width, width), F32),
            dma((2,)), dma((orbs,)), dma((orbs,)),
            dma((2, chips, half)), dma((2, chips, half)), dma((2, chips, half)), dma((2, chips, half)),
            dma((n - 1,)), dma((n - 1,)), dma((n - 1,)), dma((n - 1,)), dma((2, 3, rows)),
        ],
        compiler_params=pltpu.CompilerParams(collective_id=0, has_side_effects=True, vmem_limit_bytes=VMEM_LIMIT),
    )(first_local, fetch_local, row_pair, occ, x, pno, levels)


def group_of(pairs):
    return next(g for g in (4, 3, 2, 1) if pairs % g == 0)


def density_kernel(group, first_s, slot_s, second_s, fresh_s, final_s, seen_s, row_s,
                   shift_s, pno_ref, level_ref, *rest):
    fp_refs, sp_refs, c_refs = rest[:group], rest[group:2 * group], rest[2 * group:3 * group]
    amp_ref, dens_ref, terms_ref, acc, stage, blank, busy, stage_sem, blank_sem = rest[3 * group:]
    step = pl.program_id(0)
    width = pno_ref.shape[1]
    aux = fp_refs[0].shape[2]
    total = terms_ref.shape[0]

    def blank_copy(o):
        return pltpu.make_async_copy(blank, terms_ref.at[o], blank_sem.at[0])

    @pl.when(step == 0)
    def _():
        dens_ref[...] = jnp.zeros_like(dens_ref)
        blank[...] = jnp.zeros_like(blank)
        for j in range(group):
            busy[j] = 0

        @pl.loop(0, total)
        def _(o):
            @pl.when(seen_s[o] == 0)
            def _():
                blank_copy(o).start()

    halves = []
    for j in range(group):
        p = step * group + j
        levels = jnp.broadcast_to(level_ref[pl.ds(p, 1), :], (width, width))
        s1, s2, occ = shift_s[0, row_s[p]], shift_s[1, row_s[p]], shift_s[2, row_s[p]]
        inverse = 1.0 / (levels + levels.T - occ)
        amp = -c_refs[j][0] * inverse * (1.0 - s2 * inverse * (1.0 - s1 * inverse))
        amp_ref[j] = amp
        halves.append(amp.astype(BF16))
    parts = []
    for j in range(group):
        part1 = jnp.dot(halves[j], sp_refs[j][0], preferred_element_type=F32).astype(BF16)
        part2 = lax.dot_general(halves[j], fp_refs[j][0], (((0,), (0,)), ((), ())), preferred_element_type=F32).astype(BF16)
        parts.append(jnp.concatenate([part1, part2], axis=1))
    for j in range(group):
        p = step * group + j
        slot = slot_s[p]
        pao = lax.dot_general(pno_ref[j], parts[j], (((0,), (0,)), ((), ())), preferred_element_type=F32)
        dens_ref[first_s[p]] += pao[:, :aux]
        term = pao[:, aux:]
        acc[slot] = jnp.where(fresh_s[p] == 1, term, acc[slot] + term)

    for j in range(group):
        p = step * group + j
        sg, slot = second_s[p], slot_s[p]

        @pl.when(final_s[p] == 1)
        def _():
            copy = pltpu.make_async_copy(stage.at[j], terms_ref.at[sg], stage_sem.at[j])

            @pl.when(busy[j] == 1)
            def _():
                copy.wait()

            stage[j] = acc[slot].astype(BF16)
            copy.start()
            busy[j] = 1

    @pl.when(step == pl.num_programs(0) - 1)
    def _():
        for j in range(group):
            @pl.when(busy[j] == 1)
            def _():
                pltpu.make_async_copy(stage.at[j], terms_ref.at[0], stage_sem.at[j]).wait()

        @pl.loop(0, total)
        def _(o):
            @pl.when(seen_s[o] == 0)
            def _():
                blank_copy(o).wait()


def density_call(scalars, shifts, orbs, slots, orb_total, pno, levels, fp, sp, c):
    pairs, width, nvirt = pno.shape
    aux = fp.shape[2]
    group = group_of(pairs)
    three = lambda i, *_: (i, 0, 0)

    def row_map(j, i, *scalars):
        return (scalars[-1][i * group + j], 0, 0)

    def picked(array):
        return [pl.BlockSpec((1,) + array.shape[1:], functools.partial(row_map, j)) for j in range(group)]

    smem = pl.BlockSpec(memory_space=pltpu.SMEM)
    dma = pltpu.SemaphoreType.DMA
    return pl.pallas_call(
        functools.partial(density_kernel, group),
        name="density_terms",
        out_shape=(
            jax.ShapeDtypeStruct((pairs, width, width), F32),
            jax.ShapeDtypeStruct((orbs, nvirt, aux), F32),
            jax.ShapeDtypeStruct((orb_total, nvirt, aux), BF16),
        ),
        grid_spec=pltpu.PrefetchScalarGridSpec(
            num_scalar_prefetch=7,
            grid=(pairs // group,),
            in_specs=[
                smem,
                pl.BlockSpec((group, width, nvirt), three),
                pl.BlockSpec(levels.shape, lambda i, *_: (0, 0)),
            ] + picked(fp) + picked(sp) + picked(c),
            out_specs=(
                pl.BlockSpec((group, width, width), three),
                pl.BlockSpec((orbs, nvirt, aux), lambda i, *_: (0, 0, 0)),
                pl.BlockSpec(memory_space=pl.ANY),
            ),
            scratch_shapes=[
                pltpu.VMEM((slots, nvirt, aux), F32),
                pltpu.VMEM((group, nvirt, aux), BF16),
                pltpu.VMEM((nvirt, aux), BF16),
                pltpu.SMEM((group,), jnp.int32),
                dma((group,)), dma((1,)),
            ],
        ),
        compiler_params=pltpu.CompilerParams(vmem_limit_bytes=VMEM_LIMIT),
    )(*scalars, shifts, pno, levels, *([fp] * group + [sp] * group + [c] * group))


def home_kernel(n, terms_ref, dens_ref, out_ref, own, side, got, own_sem, side_send, side_recv, ring_send, ring_recv):
    me, chips, core, place, dev = ring(n)
    orbs, rows = dens_ref.shape[0], dens_ref.shape[1]
    half = orbs // 2
    sibling = me + 1 - 2 * core
    ends = (dev(place + 1, core), dev(place - 1, core))
    greet([ends[0], ends[1], sibling])
    chunk = 32

    def position(way, step):
        return place - 1 - step if way == 0 else place + 1 + step

    def own_copy(way, step, k):
        r = dev(position(way, step), core) * orbs + way * half + k
        return pltpu.make_async_copy(terms_ref.at[r], own.at[way, step, k], own_sem.at[way, step, k])

    def side_copy(way, step, k):
        r = dev(position(way, step), 1 - core) * orbs + way * half + k
        return remote(terms_ref.at[r], side.at[way, step, k], side_send.at[way, step, k], side_recv.at[way, step, k], sibling)

    def load(step):
        for k in range(half):
            for way in range(2):
                side_copy(way, step, k).start()
                own_copy(way, step, k).start()

    def ring_copy(way, step, k):
        return remote(side.at[way, step, k], got.at[way, step, k], ring_send.at[way, step, k], ring_recv.at[way, step, k], ends[way])

    load(0)
    load(1)
    for step in range(chips):
        for k in range(half):
            for way in range(2):
                own_copy(way, step, k).wait()
                side_copy(way, step, k).wait_recv()
                if step > 0:
                    ring_copy(way, step - 1, k).wait_recv()

                @pl.loop(0, rows // chunk)
                def _(i):
                    at = pl.ds(pl.multiple_of(i * chunk, chunk), chunk)
                    total = own[way, step, k, at, :].astype(F32) + side[way, step, k, at, :].astype(F32)
                    if step > 0:
                        total = total + got[way, step - 1, k, at, :].astype(F32)
                    if step < chips - 1:
                        side[way, step, k, at, :] = total.astype(BF16)
                    else:
                        out_ref[way * half + k, at, :] = dens_ref[way * half + k, at, :] + total

                if step < chips - 1:
                    ring_copy(way, step, k).start()
        if step + 2 < chips:
            load(step + 2)
    for step in range(chips):
        for k in range(half):
            for way in range(2):
                side_copy(way, step, k).wait_send()
                if step < chips - 1:
                    ring_copy(way, step, k).wait_send()


def home(n, terms, density):
    orbs, nvirt, aux = density.shape
    chips, half = n // 2, orbs // 2
    dma = pltpu.SemaphoreType.DMA
    many = (2, chips, half)
    return pl.pallas_call(
        functools.partial(home_kernel, n),
        name="terms_home",
        out_shape=jax.ShapeDtypeStruct(density.shape, F32),
        in_specs=[pl.BlockSpec(memory_space=pl.ANY), pl.BlockSpec(memory_space=pltpu.VMEM)],
        out_specs=pl.BlockSpec(memory_space=pltpu.VMEM),
        scratch_shapes=[
            pltpu.VMEM(many + (nvirt, aux), BF16),
            pltpu.VMEM(many + (nvirt, aux), BF16),
            pltpu.VMEM((2, chips - 1, half, nvirt, aux), BF16),
            dma(many), dma(many), dma(many), dma(many), dma(many),
        ],
        compiler_params=pltpu.CompilerParams(collective_id=2, has_side_effects=True, vmem_limit_bytes=VMEM_LIMIT),
    )(terms, density)


def on_device(orb_blocks, pno, pno_levels, occ_levels, pair_i_local, fetch_local, pair_slot):
    n = lax.axis_size("orb")
    orbs = orb_blocks.shape[0]
    pairs = pno.shape[0]
    slots = fetch_local.shape[0]
    orb_total = orbs * n
    per_owner = slots // n
    slot_of = pair_slot[:, 0]
    slot_ids = jnp.arange(slots, dtype=jnp.int32)
    pair_ids = jnp.arange(pairs, dtype=jnp.int32)
    slot_orb = slot_ids // per_owner * orbs + fetch_local
    second = jnp.sum(jnp.where(slot_of[:, None] == slot_ids[None, :], slot_orb[None, :], 0), axis=1)
    same = slot_of[:, None] == slot_of[None, :]
    fresh = 1 - jnp.any(same & (pair_ids[None, :] < pair_ids[:, None]), axis=1).astype(jnp.int32)
    final = 1 - jnp.any(same & (pair_ids[None, :] > pair_ids[:, None]), axis=1).astype(jnp.int32)
    seen = jnp.any(second[:, None] == jnp.arange(orb_total, dtype=jnp.int32)[None, :], axis=0).astype(jnp.int32)
    rank = jnp.sum((same & (pair_ids[None, :] < pair_ids[:, None])).astype(jnp.int32), axis=1)
    row_of = slot_of * MOST + rank
    row_ids = jnp.arange(slots * MOST, dtype=jnp.int32)
    row_pair = jnp.max(jnp.where(row_of[None, :] == row_ids[:, None], pair_ids[None, :], -1), axis=1)
    fp, sp, coulomb, pair_shifts = gather(
        n, pair_i_local, fetch_local, row_pair, occ_levels, orb_blocks, pno, pno_levels
    )
    scalars = (pair_i_local, slot_of, second, fresh, final, seen, row_of)
    amplitude, density, terms = density_call(
        scalars, pair_shifts, orbs, slots, orb_total, pno, pno_levels, fp, sp, coulomb
    )
    return (amplitude, home(n, terms, density))


def solution(mesh):
    placed = (
        P(("image", "orb"), None, None),
        P(("image", "orb"), None, None),
        P(("image", "orb"), None),
        P(("image", "orb")),
        P(("image", "orb")),
        P(("image", "orb")),
        P(("image", "orb"), None),
    )
    return jax.shard_map(
        on_device,
        mesh=mesh,
        in_specs=placed,
        out_specs=(P(("image", "orb"), None, None), P(("image", "orb"), None, None)),
        check_vma=False,
    )
```

```python
import functools

import jax
import jax.numpy as jnp
from jax import lax
from jax.experimental import pallas as pl
from jax.experimental.pallas import tpu as pltpu
from jax.sharding import PartitionSpec as P

MOST = 3
ITERS = 2
shift_weight = 0.1
MESH = pl.DeviceIdType.MESH
F32 = jnp.float32
BF16 = jnp.bfloat16
VMEM_LIMIT = 56 * 1024 * 1024


def chip_at(position, chips):
    position = lax.rem(position + 2 * chips, chips)
    if chips == 8:
        far = position // 4
        return 2 * (position + far * (7 - 2 * position)) + far
    return position


def place_of(chip, chips):
    if chips == 8:
        y = lax.rem(chip, 2)
        z = chip // 2
        return z + y * (7 - 2 * z)
    return chip


def ring(n):
    me = lax.axis_index("orb")
    chips = n // 2
    core = lax.rem(me, 2)
    place = place_of(me // 2, chips)

    def dev(position, c):
        return chip_at(position, chips) * 2 + c

    return me, chips, core, place, dev


def greet(others):
    barrier = pltpu.get_barrier_semaphore()
    for other in others:
        pl.semaphore_signal(barrier, inc=1, device_id={"orb": other}, device_id_type=MESH)
    pl.semaphore_wait(barrier, len(others))


def remote(src, dst, send, recv, target):
    return pltpu.make_async_remote_copy(
        src_ref=src, dst_ref=dst, send_sem=send, recv_sem=recv, device_id={"orb": target}, device_id_type=MESH
    )


def shifts(n, orb_total, e_ref, got, out_ref):
    ids = lax.broadcasted_iota(jnp.int32, (orb_total, 128), 0).astype(F32)

    def shares(block):
        return jnp.where(ids == block[2:3, :], 1.0, 0.0) + jnp.where(ids == block[3:4, :], 1.0, 0.0)

    total = jnp.zeros((orb_total, 128), F32)
    for d in range(n):
        block = got[d]
        total = total + shares(block) * block[0:1, :]
    shift = shift_weight * jnp.sum(total, axis=1, keepdims=True)
    total = jnp.zeros((orb_total, 128), F32)
    for d in range(n):
        block = got[d]
        hot = shares(block)
        pair_shift = jnp.sum(hot * shift, axis=0, keepdims=True)
        total = total + hot * (block[0:1, :] - pair_shift * block[1:2, :])
    shift2 = shift_weight * jnp.sum(total, axis=1, keepdims=True)
    mine = shares(e_ref[...])
    out_ref[...] = jnp.zeros_like(out_ref)
    out_ref[0:1, :] = jnp.sum(mine * shift, axis=0, keepdims=True)
    out_ref[1:2, :] = jnp.sum(mine * shift2, axis=0, keepdims=True)
    out_ref[2:3, :] = e_ref[4:5, :]


def gather_kernel(n, per_owner, first_s, fetch_s, row_s, occ_s, x_ref, pno_in, level_ref,
                  fp_out, sp_out, c_out, shift_ref,
                  pno_ref, info_ref, info_out, e_ref, got, blocks, moments, fp_stage, sp_stage, c_stage,
                  own_sem, first_send, first_recv, ring_send, ring_recv, side_send, side_recv, info_send, info_recv, e_send, e_recv, out_sem):
    me, chips, core, place, dev = ring(n)
    orbs = x_ref.shape[0]
    half = orbs // 2
    width = pno_ref.shape[1]
    rows = per_owner * MOST
    scale = x_ref.shape[2] ** -0.5
    norm = -1.0 / (width * width)
    sibling = me + 1 - 2 * core
    ends = (dev(place + 1, core), dev(place - 1, core))
    lane = lax.broadcasted_iota(jnp.int32, (1, 128), 1)
    pno_copy = pltpu.make_async_copy(pno_in, pno_ref, own_sem.at[1])
    pno_copy.start()
    levels_row = jnp.zeros((8, 128), F32)
    for l in range(orbs):
        levels_row = jnp.where(lane == l, occ_s[l], levels_row)
    info_ref[...] = levels_row
    greet([lax.rem(me + d, n) for d in range(1, n)])

    def owner_at(way, step):
        return dev(place - step if way == 0 else place + step, way)

    def first_copy(k):
        local = lax.rem(half * (1 - core) + k, orbs)
        return remote(x_ref.at[local], blocks.at[me, local], first_send.at[k], first_recv.at[k], sibling)

    def ring_copy(way, step, k):
        block = blocks.at[owner_at(way, step - 1), half * core + k]
        return remote(block, block, ring_send.at[way, step, k], ring_recv.at[way, step, k], ends[way])

    def ring_wait(way, step, k):
        block = blocks.at[owner_at(way, step), half * core + k]
        remote(block, block, ring_send.at[way, step, k], ring_recv.at[way, step, k], ends[way]).wait_recv()

    def side_copy(way, step, k):
        block = blocks.at[owner_at(way, step), half * core + k]
        return remote(block, block, side_send.at[way, step, k], side_recv.at[way, step, k], sibling)

    def side_wait(way, step, k):
        block = blocks.at[owner_at(way, step), half * (1 - core) + k]
        remote(block, block, side_send.at[way, step, k], side_recv.at[way, step, k], sibling).wait_recv()

    def note(d):
        return remote(info_ref, info_out.at[me], info_send.at[d - 1], info_recv.at[d - 1], lax.rem(me + d, n))

    def out_copies(way, owner, i):
        row = owner * rows + i
        return [
            pltpu.make_async_copy(stage.at[way, i], out.at[row], out_sem.at[way, kind, i])
            for kind, (stage, out) in enumerate(((fp_stage, fp_out), (sp_stage, sp_out), (c_stage, c_out)))
        ]

    def work(way, step):
        owner = owner_at(way, step)
        for s in range(per_owner):
            local = fetch_s[owner * per_owner + s]
            block = blocks[owner, 0]
            for other in range(1, orbs):
                block = jnp.where(local == other, blocks[owner, other], block)
            occ2 = jnp.sum(jnp.where(lane == local, info_out[owner, 0:1, :], 0.0), axis=1, keepdims=True)
            base = owner * rows + s * MOST
            named = [row_s[base + m] for m in range(MOST)]
            pair = [jnp.maximum(q, 0) for q in named]
            first = [first_s[q] for q in pair]
            w = [pno_ref[q] for q in pair]
            inverse, occ = [], []
            for m in range(MOST):
                levels = jnp.broadcast_to(level_ref[pl.ds(pair[m], 1), :], (width, width))
                occ1 = jnp.sum(jnp.where(lane == first[m], info_ref[0:1, :], 0.0), axis=1, keepdims=True)
                occ.append(occ1 + occ2)
                inverse.append(1.0 / (levels + levels.T - occ[m]))
            sp = [jnp.dot(w[m], block, preferred_element_type=F32).astype(BF16) for m in range(MOST)]
            fp = [jnp.dot(w[m], x_ref[first[m]], preferred_element_type=F32).astype(BF16) for m in range(MOST)]
            c = [
                lax.dot_general(fp[m], sp[m], (((1,), (1,)), ((), ())), preferred_element_type=F32) * scale
                for m in range(MOST)
            ]
            t = [c[m] * (2.0 * c[m] - c[m].T) * inverse[m] for m in range(MOST)]
            for m in range(MOST):
                i = s * MOST + m
                fp_stage[way, i] = fp[m]
                sp_stage[way, i] = sp[m]
                c_stage[way, i] = c[m]
                moments[0, pl.ds(base + m, 1), :] = jnp.sum(t[m], axis=0, keepdims=True)
                moments[1, pl.ds(base + m, 1), :] = jnp.sum(t[m] * inverse[m], axis=0, keepdims=True)
                here = lane == base + m
                id1 = jnp.where(named[m] >= 0, me * orbs + first[m], -1).astype(F32)
                id2 = jnp.where(named[m] >= 0, owner * orbs + local, -1).astype(F32)
                e_ref[2:3, :] = jnp.where(here, id1, e_ref[2:3, :])
                e_ref[3:4, :] = jnp.where(here, id2, e_ref[3:4, :])
                e_ref[4:5, :] = jnp.where(here, occ[m], e_ref[4:5, :])
        for i in range(rows):
            for copy in out_copies(way, owner, i):
                copy.start()

    for k in range(orbs):
        first_copy(k).start()
    own = pltpu.make_async_copy(x_ref, blocks.at[me], own_sem.at[0])
    own.start()
    own.wait()
    for k in range(half):
        first_copy(k).wait_recv()
    for k in range(half):
        for way in range(2):
            ring_copy(way, 1, k).start()
    for d in range(1, n):
        note(d).start()
    info_out[me] = info_ref[...]
    e_ref[...] = jnp.zeros_like(e_ref)
    e_ref[2:4, :] = jnp.full((2, 128), -1.0, F32)
    moments[...] = jnp.zeros_like(moments)
    for k in range(half, orbs):
        first_copy(k).wait_recv()
    for d in range(1, n):
        note(d).wait()
    pno_copy.wait()

    def turn(step, carry):
        for k in range(half):
            for way in range(2):
                if way % half == k:
                    @pl.when(step > 1)
                    def _():
                        for kk in range(half):
                            side_wait(way, step - 1, kk)
                        for i in range(rows):
                            for copy in out_copies(way, owner_at(way, step - 2), i):
                                copy.wait()

                    work(way, step - 1)

            @pl.when(step < chips)
            def _():
                for way in range(2):
                    ring_wait(way, step, k)

                    @pl.when(step < chips - 1)
                    def _():
                        ring_copy(way, step + 1, k).start()

                    side_copy(way, step, k).start()
        return carry

    lax.fori_loop(1, chips + 1, turn, 0)
    square = lax.broadcasted_iota(jnp.int32, (128, 128), 0) == lax.broadcasted_iota(jnp.int32, (128, 128), 1)
    for kind in range(2):
        column = jnp.sum(moments[kind], axis=1, keepdims=True) * norm
        e_ref[kind:kind + 1, :] = jnp.sum(jnp.where(square, column, 0.0), axis=0, keepdims=True)

    def energy_copy(d):
        return remote(e_ref, got.at[me], e_send.at[d - 1], e_recv.at[d - 1], lax.rem(me + d, n))

    for d in range(1, n):
        energy_copy(d).start()
    got[me] = e_ref[...]
    for d in range(1, n):
        energy_copy(d).wait()
    shifts(n, n * orbs, e_ref, got, shift_ref)
    for way in range(2):
        for i in range(rows):
            for copy in out_copies(way, owner_at(way, chips - 1), i):
                copy.wait()
    for k in range(orbs):
        first_copy(k).wait_send()

    def drain(step, carry):
        for k in range(half):
            for way in range(2):
                ring_copy(way, step, k).wait_send()
                side_copy(way, step, k).wait_send()
        return carry

    lax.fori_loop(1, chips, drain, 0)


def gather(n, first_local, fetch_local, row_pair, occ, x, pno, levels):
    pairs, width, nvirt = pno.shape
    orbs, _, aux = x.shape
    per_owner = fetch_local.shape[0] // n
    rows = per_owner * MOST
    total = rows * n
    chips, half = n // 2, orbs // 2
    dma = pltpu.SemaphoreType.DMA
    smem, vmem, anywhere = (pl.BlockSpec(memory_space=m) for m in (pltpu.SMEM, pltpu.VMEM, pl.ANY))
    return pl.pallas_call(
        functools.partial(gather_kernel, n, per_owner),
        name="gather_coulomb",
        out_shape=(
            jax.ShapeDtypeStruct((total, width, aux), BF16),
            jax.ShapeDtypeStruct((total, width, aux), BF16),
            jax.ShapeDtypeStruct((total, width, width), F32),
            jax.ShapeDtypeStruct((8, 128), F32),
        ),
        in_specs=[smem, smem, smem, smem, vmem, anywhere, vmem],
        out_specs=(anywhere, anywhere, anywhere, vmem),
        scratch_shapes=[
            pltpu.VMEM(pno.shape, BF16),
            pltpu.VMEM((8, 128), F32),
            pltpu.VMEM((n, 8, 128), F32),
            pltpu.VMEM((8, 128), F32),
            pltpu.VMEM((n, 8, 128), F32),
            pltpu.VMEM((n, orbs, nvirt, aux), BF16),
            pltpu.VMEM((2, 128, width), F32),
            pltpu.VMEM((2, rows, width, aux), BF16),
            pltpu.VMEM((2, rows, width, aux), BF16),
            pltpu.VMEM((2, rows, width, width), F32),
            dma((2,)), dma((orbs,)), dma((orbs,)),
            dma((2, chips, half)), dma((2, chips, half)), dma((2, chips, half)), dma((2, chips, half)),
            dma((n - 1,)), dma((n - 1,)), dma((n - 1,)), dma((n - 1,)), dma((2, 3, rows)),
        ],
        compiler_params=pltpu.CompilerParams(collective_id=0, has_side_effects=True, vmem_limit_bytes=VMEM_LIMIT),
    )(first_local, fetch_local, row_pair, occ, x, pno, levels)


def group_of(pairs):
    return next(g for g in (4, 3, 2, 1) if pairs % g == 0)


def density_kernel(group, first_s, slot_s, second_s, fresh_s, final_s, seen_s, row_s,
                   shift_s, pno_ref, level_ref, *rest):
    fp_refs, sp_refs, c_refs = rest[:group], rest[group:2 * group], rest[2 * group:3 * group]
    amp_ref, dens_ref, terms_ref, acc, stage, blank, busy, stage_sem, blank_sem = rest[3 * group:]
    step = pl.program_id(0)
    width = pno_ref.shape[1]
    aux = fp_refs[0].shape[2]
    total = terms_ref.shape[0]

    def blank_copy(o):
        return pltpu.make_async_copy(blank, terms_ref.at[o], blank_sem.at[0])

    @pl.when(step == 0)
    def _():
        dens_ref[...] = jnp.zeros_like(dens_ref)
        blank[...] = jnp.zeros_like(blank)
        for j in range(group):
            busy[j] = 0

        @pl.loop(0, total)
        def _(o):
            @pl.when(seen_s[o] == 0)
            def _():
                blank_copy(o).start()

    halves = []
    for j in range(group):
        p = step * group + j
        levels = jnp.broadcast_to(level_ref[pl.ds(p, 1), :], (width, width))
        s1, s2, occ = shift_s[0, row_s[p]], shift_s[1, row_s[p]], shift_s[2, row_s[p]]
        inverse = 1.0 / (levels + levels.T - occ)
        amp = -c_refs[j][0] * inverse * (1.0 - s2 * inverse * (1.0 - s1 * inverse))
        amp_ref[j] = amp
        halves.append(amp.astype(BF16))
    parts = []
    for j in range(group):
        part1 = jnp.dot(halves[j], sp_refs[j][0], preferred_element_type=F32).astype(BF16)
        part2 = lax.dot_general(halves[j], fp_refs[j][0], (((0,), (0,)), ((), ())), preferred_element_type=F32).astype(BF16)
        parts.append(jnp.concatenate([part1, part2], axis=1))
    for j in range(group):
        p = step * group + j
        slot = slot_s[p]
        pao = lax.dot_general(pno_ref[j], parts[j], (((0,), (0,)), ((), ())), preferred_element_type=F32)
        dens_ref[first_s[p]] += pao[:, :aux]
        term = pao[:, aux:]
        acc[slot] = jnp.where(fresh_s[p] == 1, term, acc[slot] + term)

    for j in range(group):
        p = step * group + j
        sg, slot = second_s[p], slot_s[p]

        @pl.when(final_s[p] == 1)
        def _():
            copy = pltpu.make_async_copy(stage.at[j], terms_ref.at[sg], stage_sem.at[j])

            @pl.when(busy[j] == 1)
            def _():
                copy.wait()

            stage[j] = acc[slot].astype(BF16)
            copy.start()
            busy[j] = 1

    @pl.when(step == pl.num_programs(0) - 1)
    def _():
        for j in range(group):
            @pl.when(busy[j] == 1)
            def _():
                pltpu.make_async_copy(stage.at[j], terms_ref.at[0], stage_sem.at[j]).wait()

        @pl.loop(0, total)
        def _(o):
            @pl.when(seen_s[o] == 0)
            def _():
                blank_copy(o).wait()


def density_call(scalars, shifts, orbs, slots, orb_total, pno, levels, fp, sp, c):
    pairs, width, nvirt = pno.shape
    aux = fp.shape[2]
    group = group_of(pairs)
    three = lambda i, *_: (i, 0, 0)

    def row_map(j, i, *scalars):
        return (scalars[-1][i * group + j], 0, 0)

    def picked(array):
        return [pl.BlockSpec((1,) + array.shape[1:], functools.partial(row_map, j)) for j in range(group)]

    smem = pl.BlockSpec(memory_space=pltpu.SMEM)
    dma = pltpu.SemaphoreType.DMA
    return pl.pallas_call(
        functools.partial(density_kernel, group),
        name="density_terms",
        out_shape=(
            jax.ShapeDtypeStruct((pairs, width, width), F32),
            jax.ShapeDtypeStruct((orbs, nvirt, aux), F32),
            jax.ShapeDtypeStruct((orb_total, nvirt, aux), BF16),
        ),
        grid_spec=pltpu.PrefetchScalarGridSpec(
            num_scalar_prefetch=7,
            grid=(pairs // group,),
            in_specs=[
                smem,
                pl.BlockSpec((group, width, nvirt), three),
                pl.BlockSpec(levels.shape, lambda i, *_: (0, 0)),
            ] + picked(fp) + picked(sp) + picked(c),
            out_specs=(
                pl.BlockSpec((group, width, width), three),
                pl.BlockSpec((orbs, nvirt, aux), lambda i, *_: (0, 0, 0)),
                pl.BlockSpec(memory_space=pl.ANY),
            ),
            scratch_shapes=[
                pltpu.VMEM((slots, nvirt, aux), F32),
                pltpu.VMEM((group, nvirt, aux), BF16),
                pltpu.VMEM((nvirt, aux), BF16),
                pltpu.SMEM((group,), jnp.int32),
                dma((group,)), dma((1,)),
            ],
        ),
        compiler_params=pltpu.CompilerParams(vmem_limit_bytes=VMEM_LIMIT),
    )(*scalars, shifts, pno, levels, *([fp] * group + [sp] * group + [c] * group))


def home_kernel(n, terms_ref, dens_ref, out_ref, own, side, got, own_sem, side_send, side_recv, ring_send, ring_recv):
    me, chips, core, place, dev = ring(n)
    orbs, rows = dens_ref.shape[0], dens_ref.shape[1]
    half = orbs // 2
    sibling = me + 1 - 2 * core
    ends = (dev(place + 1, core), dev(place - 1, core))
    chunk = 32

    def position(way, step):
        return place - 1 - step if way == 0 else place + 1 + step

    def own_copy(way, step, k):
        r = dev(position(way, step), core) * orbs + way * half + k
        return pltpu.make_async_copy(terms_ref.at[r], own.at[way, step, k], own_sem.at[way, step, k])

    def side_copy(way, step, k):
        r = dev(position(way, step), 1 - core) * orbs + way * half + k
        return remote(terms_ref.at[r], side.at[way, step, k], side_send.at[way, step, k], side_recv.at[way, step, k], sibling)

    def load_own(step):
        for k in range(half):
            for way in range(2):
                own_copy(way, step, k).start()

    def load_side(step):
        for k in range(half):
            for way in range(2):
                side_copy(way, step, k).start()

    def ring_copy(way, step, k):
        return remote(side.at[way, step, k], got.at[way, step, k], ring_send.at[way, step, k], ring_recv.at[way, step, k], ends[way])

    load_own(0)
    load_own(1)
    greet([ends[0], ends[1], sibling])
    load_side(0)
    load_side(1)
    for step in range(chips):
        for k in range(half):
            for way in range(2):
                own_copy(way, step, k).wait()
                side_copy(way, step, k).wait_recv()
                if step > 0:
                    ring_copy(way, step - 1, k).wait_recv()

                @pl.loop(0, rows // chunk)
                def _(i):
                    at = pl.ds(pl.multiple_of(i * chunk, chunk), chunk)
                    total = own[way, step, k, at, :].astype(F32) + side[way, step, k, at, :].astype(F32)
                    if step > 0:
                        total = total + got[way, step - 1, k, at, :].astype(F32)
                    if step < chips - 1:
                        side[way, step, k, at, :] = total.astype(BF16)
                    else:
                        out_ref[way * half + k, at, :] = dens_ref[way * half + k, at, :] + total

                if step < chips - 1:
                    ring_copy(way, step, k).start()
        if step + 2 < chips:
            load_side(step + 2)
            load_own(step + 2)
    for step in range(chips):
        for k in range(half):
            for way in range(2):
                side_copy(way, step, k).wait_send()
                if step < chips - 1:
                    ring_copy(way, step, k).wait_send()


def home(n, terms, density):
    orbs, nvirt, aux = density.shape
    chips, half = n // 2, orbs // 2
    dma = pltpu.SemaphoreType.DMA
    many = (2, chips, half)
    return pl.pallas_call(
        functools.partial(home_kernel, n),
        name="terms_home",
        out_shape=jax.ShapeDtypeStruct(density.shape, F32),
        in_specs=[pl.BlockSpec(memory_space=pl.ANY), pl.BlockSpec(memory_space=pltpu.VMEM)],
        out_specs=pl.BlockSpec(memory_space=pltpu.VMEM),
        scratch_shapes=[
            pltpu.VMEM(many + (nvirt, aux), BF16),
            pltpu.VMEM(many + (nvirt, aux), BF16),
            pltpu.VMEM((2, chips - 1, half, nvirt, aux), BF16),
            dma(many), dma(many), dma(many), dma(many), dma(many),
        ],
        compiler_params=pltpu.CompilerParams(collective_id=2, has_side_effects=True, vmem_limit_bytes=VMEM_LIMIT),
    )(terms, density)


def on_device(orb_blocks, pno, pno_levels, occ_levels, pair_i_local, fetch_local, pair_slot):
    n = lax.axis_size("orb")
    orbs = orb_blocks.shape[0]
    pairs = pno.shape[0]
    slots = fetch_local.shape[0]
    orb_total = orbs * n
    per_owner = slots // n
    slot_of = pair_slot[:, 0]
    slot_ids = jnp.arange(slots, dtype=jnp.int32)
    pair_ids = jnp.arange(pairs, dtype=jnp.int32)
    slot_orb = slot_ids // per_owner * orbs + fetch_local
    second = jnp.sum(jnp.where(slot_of[:, None] == slot_ids[None, :], slot_orb[None, :], 0), axis=1)
    same = slot_of[:, None] == slot_of[None, :]
    fresh = 1 - jnp.any(same & (pair_ids[None, :] < pair_ids[:, None]), axis=1).astype(jnp.int32)
    final = 1 - jnp.any(same & (pair_ids[None, :] > pair_ids[:, None]), axis=1).astype(jnp.int32)
    seen = jnp.any(second[:, None] == jnp.arange(orb_total, dtype=jnp.int32)[None, :], axis=0).astype(jnp.int32)
    rank = jnp.sum((same & (pair_ids[None, :] < pair_ids[:, None])).astype(jnp.int32), axis=1)
    row_of = slot_of * MOST + rank
    row_ids = jnp.arange(slots * MOST, dtype=jnp.int32)
    row_pair = jnp.max(jnp.where(row_of[None, :] == row_ids[:, None], pair_ids[None, :], -1), axis=1)
    fp, sp, coulomb, pair_shifts = gather(
        n, pair_i_local, fetch_local, row_pair, occ_levels, orb_blocks, pno, pno_levels
    )
    scalars = (pair_i_local, slot_of, second, fresh, final, seen, row_of)
    amplitude, density, terms = density_call(
        scalars, pair_shifts, orbs, slots, orb_total, pno, pno_levels, fp, sp, coulomb
    )
    return (amplitude, home(n, terms, density))


def solution(mesh):
    placed = (
        P(("image", "orb"), None, None),
        P(("image", "orb"), None, None),
        P(("image", "orb"), None),
        P(("image", "orb")),
        P(("image", "orb")),
        P(("image", "orb")),
        P(("image", "orb"), None),
    )
    return jax.shard_map(
        on_device,
        mesh=mesh,
        in_specs=placed,
        out_specs=(P(("image", "orb"), None, None), P(("image", "orb"), None, None)),
        check_vma=False,
    )
```
